32 devices in a mesh: member: 2 (over x), node: 16 (over z, y, core).
Axes of the slice: x: 2, y: 2, z: 4, core: 2. Of those that a mesh axis runs over, the one named last changes fastest.
Arguments:
- vertex_embedding_array: bfloat16 [2, 65536, 128], P('member', 'node'), may hold values from -12 to 12
- result_sensitivity: bfloat16 [2, 65536, 128], P('member', 'node'), may hold values from -6 to 6
- hidden_projection: bfloat16 [128, 128], replicated, may hold values from -0.5 to 0.5
- aggregate_projection: bfloat16 [128, 128], replicated, may hold values from -0.5 to 0.5
- aggregate_offset: float32 [128], replicated, may hold values from -3 to 3
- assignment_projection: bfloat16 [16, 32], replicated, may hold values from -1.5 to 1.5
- softmax_sharpness: float32 [8], replicated, may hold values from 0.5 to 2
- state_asking_map: bfloat16 [16, 16], replicated, may hold values from -1.5 to 1.5
- state_lookup_map: bfloat16 [16, 16], replicated, may hold values from -1.5 to 1.5
- state_content_map: bfloat16 [16, 16], replicated, may hold values from -1.5 to 1.5
- result_projection: bfloat16 [128, 128], replicated, may hold values from -0.5 to 0.5
Outputs:
- vertex_sensitivity: float32 [2, 65536, 128], P('member', 'node')
- mid_grad: float32 [128, 128], replicated
- feature_grad: float32 [128, 128], replicated
- bias_grad: float32 [128], replicated
- slice_grad: float32 [16, 32], replicated
- temperature_grad: float32 [8], replicated
- query_grad: float32 [16, 16], replicated
- key_grad: float32 [16, 16], replicated
- value_grad: float32 [16, 16], replicated
- projection_grad: float32 [128, 128], replicated
The draws below stay inside these ranges and needn't reach their ends.
All inputs are finite; a program needn't handle non-finite values.
Results may differ from the reference program's by a relative error of at most 0.0054.
The reference program's roundings to bfloat16 on the way count: a program that leaves them out, or rounds other values in their place, can miss the bound.
Values sent between devices are 32-bit elements; how exact they have to be, the bound alone decides.
A program may use at most 64 MiB of HBM per device.

```python
import math
import jax
import jax.numpy as jnp
from jax import lax

MODEL_WIDTH = 128
NUM_CHANNELS = 8
M = 32
D = 16
NODES = 65536
MEMBERS = 2


def draw_vertex_embedding_array(key, part):
    subkeys = jax.random.split(key, 3)
    centres = jax.random.normal(subkeys[0], (MEMBERS, 16, MODEL_WIDTH), jnp.float32)
    labels = jax.random.randint(subkeys[1], (MEMBERS, NODES), 0, 16)
    picked = jax.vmap(lambda centre_table, label_rows: centre_table[label_rows])(centres, labels)
    jitter = jax.random.normal(subkeys[2], (MEMBERS, NODES, MODEL_WIDTH), jnp.float32)
    return jnp.clip(1.5 * picked + jitter, -12.0, 12.0).astype(jnp.bfloat16)


def shard_levels(key, dims, cuts, low, top_value):
    factor_of = 1.0
    for position, parts in cuts:
        heights = jax.random.uniform(jax.random.fold_in(jax.random.fold_in(key, 6), position), (parts,), jnp.float32, low / len(cuts), top_value / len(cuts))
        factor_of = factor_of * jnp.repeat(jnp.exp(heights), dims[position] // parts).reshape((-1,) + (1,) * (len(dims) - 1 - position))
    return factor_of


def bell_draw(own_key, dims, width, reach, shards=(), dtype=jnp.bfloat16):
    drawn = jax.random.normal(own_key, dims, jnp.float32) * width
    if len(shards) > 0:
        drawn = shard_levels(own_key, dims, shards, -0.22, 0.18) * drawn
    return jnp.clip(drawn, min=-reach, max=reach).astype(dtype)


def setup_inputs(seed: int = 0) -> dict:
    seeds = jax.random.split(jax.random.key(seed), 12)
    vertex_embedding_array = draw_vertex_embedding_array(jax.random.fold_in(seeds[11], 71), 0)
    result_sensitivity = bell_draw(seeds[1], (MEMBERS, NODES, MODEL_WIDTH), 1.0, 6.0, ((0, 2), (1, 16)))
    hidden_projection = bell_draw(seeds[2], (MODEL_WIDTH, MODEL_WIDTH), MODEL_WIDTH ** -0.5, 0.5)
    aggregate_projection = bell_draw(seeds[3], (MODEL_WIDTH, MODEL_WIDTH), MODEL_WIDTH ** -0.5, 0.5)
    aggregate_offset = bell_draw(seeds[4], (MODEL_WIDTH,), 0.5, 3.0, (), jnp.float32)
    assignment_projection = bell_draw(seeds[5], (D, M), D ** -0.5, 1.5)
    softmax_sharpness = jnp.clip(jnp.exp(jax.random.uniform(seeds[6], (NUM_CHANNELS,), jnp.float32, math.log(0.5), math.log(2.0))), 0.5, 2.0)
    state_asking_map = bell_draw(seeds[7], (D, D), D ** -0.5, 1.5)
    state_lookup_map = bell_draw(seeds[8], (D, D), D ** -0.5, 1.5)
    state_content_map = bell_draw(seeds[9], (D, D), D ** -0.5, 1.5)
    result_projection = bell_draw(seeds[10], (MODEL_WIDTH, MODEL_WIDTH), MODEL_WIDTH ** -0.5, 0.5)
    return {"vertex_embedding_array": vertex_embedding_array, "result_sensitivity": result_sensitivity, "hidden_projection": hidden_projection, "aggregate_projection": aggregate_projection, "aggregate_offset": aggregate_offset, "assignment_projection": assignment_projection, "softmax_sharpness": softmax_sharpness, "state_asking_map": state_asking_map, "state_lookup_map": state_lookup_map, "state_content_map": state_content_map, "result_projection": result_projection}


epsilon = 1e-05

def attend(physical_state_vectors, state_asking_map, state_lookup_map, state_content_map):
    exact_arithmetic_mode = lax.Precision.HIGHEST
    asking_vectors = jnp.einsum('uzi,ib->uzb', physical_state_vectors, state_asking_map, precision=exact_arithmetic_mode)
    random_seed_list = jnp.einsum('uzi,ib->uzb', physical_state_vectors, state_lookup_map, precision=exact_arithmetic_mode)
    content_vectors = jnp.einsum('uzi,ib->uzb', physical_state_vectors, state_content_map, precision=exact_arithmetic_mode)
    assignment_shares = jnp.einsum('hme,hke->hmk', asking_vectors, random_seed_list, precision=exact_arithmetic_mode) / math.sqrt(physical_state_vectors.shape[-1])
    expon = jnp.exp(assignment_shares)
    attention_rows = expon / lax.optimization_barrier(jnp.sum(expon, -1, keepdims=True))
    return jnp.einsum('lso,log->lsg', attention_rows, content_vectors, precision=exact_arithmetic_mode)

def single_ensemble_evaluation(channel_embedding, incoming_sensitivity, hidden_projection, aggregate_projection, aggregate_offset, assignment_projection, softmax_sharpness, state_asking_map, state_lookup_map, state_content_map, result_projection):
    exact_arithmetic_mode = lax.Precision.HIGHEST
    mesh_node_rows = channel_embedding.shape[0]
    mid_half = jnp.dot(channel_embedding, hidden_projection, preferred_element_type=jnp.float32).astype(jnp.bfloat16).reshape(mesh_node_rows, NUM_CHANNELS, D)
    feature_halfway = (jnp.dot(channel_embedding, aggregate_projection, preferred_element_type=jnp.float32) + aggregate_offset).astype(jnp.bfloat16).reshape(mesh_node_rows, NUM_CHANNELS, D)
    assignment_shares = jnp.einsum('nhd,dm->nhm', mid_half.astype(jnp.float32), assignment_projection.astype(jnp.float32), precision=exact_arithmetic_mode)
    assignment_energies = assignment_shares / softmax_sharpness[None, :, None]
    expon = jnp.exp(assignment_energies)
    probs = expon / lax.optimization_barrier(jnp.sum(expon, -1, keepdims=True))
    probability_halfway = probs.astype(jnp.bfloat16)
    pooled_numerator = jnp.einsum('wou,wog->oug', probability_halfway.astype(jnp.float32), feature_halfway.astype(jnp.float32), precision=exact_arithmetic_mode)
    denominator = lax.optimization_barrier(jnp.sum(probs, 0))
    physical_state_vectors = pooled_numerator / (denominator[:, :, None] + epsilon)
    token_out, attend_back = jax.vjp(attend, physical_state_vectors, state_asking_map.astype(jnp.float32), state_lookup_map.astype(jnp.float32), state_content_map.astype(jnp.float32))
    tokens_halfway = token_out.astype(jnp.bfloat16)
    mixed_tokens = jnp.einsum('afq,fqx->afx', probability_halfway.astype(jnp.float32), tokens_halfway.astype(jnp.float32), precision=exact_arithmetic_mode)
    mixed_half = mixed_tokens.reshape(mesh_node_rows, MODEL_WIDTH).astype(jnp.bfloat16)
    backward_halfway = jnp.dot(incoming_sensitivity, result_projection.T, preferred_element_type=jnp.float32).astype(jnp.bfloat16).reshape(mesh_node_rows, NUM_CHANNELS, D)
    mapping_contribution = jnp.dot(mixed_half.T, incoming_sensitivity, preferred_element_type=jnp.float32)
    slice_token_gradient = jnp.einsum('wou,wog->oug', probability_halfway.astype(jnp.float32), backward_halfway.astype(jnp.float32), precision=exact_arithmetic_mode)
    piece_reverse_derivative, asking_contribution, lookup_contribution, content_contribution = attend_back(slice_token_gradient)
    inverse = 1.0 / (denominator + epsilon)
    numerator_halfway = (piece_reverse_derivative * inverse[:, :, None]).astype(jnp.bfloat16)
    denom_back = -lax.optimization_barrier(jnp.sum(piece_reverse_derivative * physical_state_vectors, -1)) * inverse
    probability_backward = jnp.einsum('yrq,req->yre', backward_halfway.astype(jnp.float32), tokens_halfway.astype(jnp.float32), precision=exact_arithmetic_mode)
    probability_backward = probability_backward + jnp.einsum('yrq,req->yre', feature_halfway.astype(jnp.float32), numerator_halfway.astype(jnp.float32), precision=exact_arithmetic_mode)
    probability_backward = probability_backward + denom_back[None]
    feature_backward = jnp.einsum('afq,fqx->afx', probability_halfway.astype(jnp.float32), numerator_halfway.astype(jnp.float32), precision=exact_arithmetic_mode).reshape(mesh_node_rows, MODEL_WIDTH)
    shift_term_derivative = lax.optimization_barrier(jnp.sum(feature_backward, 0))
    feat_back_half = feature_backward.astype(jnp.bfloat16)
    inner = lax.optimization_barrier(jnp.sum(probs * probability_backward, -1, keepdims=True))
    assignment_energy_adjoint = probs * (probability_backward - inner)
    inverse_spread_derivative = -lax.optimization_barrier(jnp.sum(assignment_energy_adjoint * assignment_energies, axis=(0, 2))) / softmax_sharpness
    assignment_partial_result = (assignment_energy_adjoint / softmax_sharpness[None, :, None]).astype(jnp.bfloat16)
    division_term_derivative = jnp.einsum('nhd,nhm->dm', mid_half.astype(jnp.float32), assignment_partial_result.astype(jnp.float32), precision=exact_arithmetic_mode)
    mid_back_half = jnp.einsum('nhm,dm->nhd', assignment_partial_result.astype(jnp.float32), assignment_projection.astype(jnp.float32), precision=exact_arithmetic_mode).reshape(mesh_node_rows, MODEL_WIDTH).astype(jnp.bfloat16)
    hidden_contribution = jnp.dot(channel_embedding.T, mid_back_half, preferred_element_type=jnp.float32)
    channel_contribution = jnp.dot(channel_embedding.T, feat_back_half, preferred_element_type=jnp.float32)
    vertex_sensitivity = jnp.dot(mid_back_half, hidden_projection.T, preferred_element_type=jnp.float32) + jnp.dot(feat_back_half, aggregate_projection.T, preferred_element_type=jnp.float32)
    return (vertex_sensitivity, hidden_contribution, channel_contribution, shift_term_derivative, division_term_derivative, inverse_spread_derivative, asking_contribution, lookup_contribution, content_contribution, mapping_contribution)

def reference(vertex_embedding_array, result_sensitivity, hidden_projection, aggregate_projection, aggregate_offset, assignment_projection, softmax_sharpness, state_asking_map, state_lookup_map, state_content_map, result_projection):

    def one_member(layer_arguments):
        return single_ensemble_evaluation(layer_arguments[0], layer_arguments[1], hidden_projection, aggregate_projection, aggregate_offset, assignment_projection, softmax_sharpness, state_asking_map, state_lookup_map, state_content_map, result_projection)
    results = lax.map(one_member, (vertex_embedding_array, result_sensitivity))
    return (results[0], lax.optimization_barrier(jnp.sum(results[1], 0)), lax.optimization_barrier(jnp.sum(results[2], 0)), lax.optimization_barrier(jnp.sum(results[3], 0)), lax.optimization_barrier(jnp.sum(results[4], 0)), lax.optimization_barrier(jnp.sum(results[5], 0)), lax.optimization_barrier(jnp.sum(results[6], 0)), lax.optimization_barrier(jnp.sum(results[7], 0)), lax.optimization_barrier(jnp.sum(results[8], 0)), lax.optimization_barrier(jnp.sum(results[9], 0)))
```

```python
import functools
import math

import jax
import jax.numpy as jnp
from jax import lax
from jax.experimental import pallas as pl
from jax.experimental.pallas import tpu as pltpu
from jax.sharding import PartitionSpec as P

W = 128
HEADS = 8
M = 32
D = 16
S = HEADS * M
LOW = 4
CHUNK = 512
EPS = 1e-05
F32 = jnp.float32
BF16 = jnp.bfloat16
HIGHEST = lax.Precision.HIGHEST
MESH = pl.DeviceIdType.MESH

NN = (((1,), (0,)), ((), ()))
NT = (((1,), (1,)), ((), ()))
TN = (((0,), (0,)), ((), ()))


def dot(a, b, dims=NN):
    return lax.dot_general(a, b, dims, preferred_element_type=F32)


def dot32(a, b, dims=NN):
    return lax.dot_general(a, b, dims, precision=HIGHEST, preferred_element_type=F32)


def iota(shape, axis):
    return lax.broadcasted_iota(jnp.int32, shape, axis)


def group_sum(values, ones):
    upper = values.astype(BF16)
    lower = (values - upper.astype(F32)).astype(BF16)
    return dot(upper, ones) + dot(lower, ones)


def fold_rows(a, step):
    total = a[0:step]
    for i in range(step, a.shape[0], step):
        total = total + a[i : i + step]
    return total


def main_kernel(
    n_member, n_node, parts, part_rows,
    s_ref, x_hbm, g_hbm, w1_ref, w2_ref, off_ref, a_ref, wq_ref, wk_ref, wv_ref, w3_ref,
    packed_ref, mf_hbm,
    x_ref, g_ref, mid_ref, fb_ref, pb_ref, probs_ref, logits_ref, mf_ref,
    pool_acc, den_acc, xg_acc, slice_acc, proj_acc, bias_acc, temp_acc,
    pool_src, pool_recv, pool_z, pool_full, grad_src, grad_recv, grad_z, grad_full,
    in_sem, out_sem,
    a_send, a_recv, b_send, b_recv, c_send, c_recv,
    d_send, d_recv, e_send, e_recv, f_send, f_recv,
):
    rows = x_ref.shape[0]
    high_n = n_node // LOW
    member, node = lax.axis_index("member"), lax.axis_index("node")
    low, high = lax.rem(node, LOW), lax.div(node, LOW)
    group = member * LOW + low

    def low_peer(k):
        return lax.rem(low + k, LOW)

    def high_peer(k):
        return lax.rem(high + k, high_n)

    def group_peer(k):
        return lax.rem(group + k, parts)

    def low_id(k):
        return (member, high * LOW + low_peer(k))

    def high_id(k):
        return (member, high_peer(k) * LOW + low)

    def group_id(k):
        peer = group_peer(k)
        return (lax.div(peer, LOW), high * LOW + lax.rem(peer, LOW))

    load_x = pltpu.make_async_copy(x_hbm, x_ref, in_sem.at[0])
    load_g = pltpu.make_async_copy(g_hbm, g_ref, in_sem.at[1])
    load_x.start()
    load_g.start()

    barrier = pltpu.get_barrier_semaphore()
    for k in range(1, parts):
        pl.semaphore_signal(barrier, inc=1, device_id=group_id(k), device_id_type=MESH)
    for k in range(1, high_n):
        pl.semaphore_signal(barrier, inc=1, device_id=high_id(k), device_id_type=MESH)

    def send(src, dst, send_sem, recv_sem, target):
        copy = pltpu.make_async_remote_copy(
            src_ref=src, dst_ref=dst, send_sem=send_sem, recv_sem=recv_sem,
            device_id=target, device_id_type=MESH,
        )
        copy.start()
        return copy

    head_of_slice = iota((1, S), 1) // M
    inv_s = jnp.zeros((1, S), F32)
    for h in range(HEADS):
        inv_s = jnp.where(head_of_slice == h, 1.0 / jnp.full((1, S), s_ref[h], F32), inv_s)
    ones = jnp.where(iota((S, S), 0) // M == iota((S, S), 1) // M, 1.0, 0.0).astype(BF16)
    same_head = iota((W, S), 0) // D == iota((W, S), 1) // M
    pick_rows = jnp.where(iota((W, D), 0) % D == iota((W, D), 1), 1.0, 0.0).astype(BF16)
    pick_slices = jnp.where(iota((M, S), 1) % M == iota((M, S), 0), 1.0, 0.0).astype(BF16)
    pick_columns = jnp.where(iota((D, W), 1) % D == iota((D, W), 0), 1.0, 0.0).astype(BF16)
    a_all = dot(dot(pick_rows, a_ref[...]).astype(BF16), pick_slices)
    a_block = jnp.where(same_head, a_all, 0.0).astype(BF16)
    head_square = iota((W, W), 0) // D == iota((W, W), 1) // D

    def square_block(ref):
        return jnp.where(
            head_square, dot(dot(pick_rows, ref[...]).astype(BF16), pick_columns), 0.0
        )

    w12 = jnp.concatenate([w1_ref[...], w2_ref[...]], axis=1)
    w3 = w3_ref[...]
    offset = off_ref[...]

    pool_acc[...] = jnp.zeros_like(pool_acc)
    den_acc[...] = jnp.zeros_like(den_acc)
    load_x.wait()
    load_g.wait()

    def first(i, carry):
        at = pl.ds(pl.multiple_of(i * CHUNK, CHUNK), CHUNK)
        x = x_ref[at, :]
        both = dot(x, w12)
        mid = both[:, :W].astype(BF16)
        feat = (both[:, W:] + offset).astype(BF16)
        back = dot(g_ref[at, :], w3, NT).astype(BF16)
        logits = dot(mid, a_block) * inv_s
        e = jnp.exp(logits)
        probs = e / group_sum(e, ones)
        pb = probs.astype(BF16)
        fb = jnp.concatenate([back, feat], axis=1)
        mid_ref[at, :] = mid
        fb_ref[at, :] = fb
        pb_ref[at, :] = pb
        probs_ref[at, :] = probs
        logits_ref[at, :] = logits
        pool_acc[...] += dot(pb, fb, TN)
        den_acc[...] += jnp.sum(probs.reshape(CHUNK // 8, 8, S), axis=0)
        return carry

    lax.fori_loop(0, rows // CHUNK, first, 0)

    slice_head = iota((S, W), 0) // M == iota((S, W), 1) // D
    token_grad = fold_rows(jnp.where(slice_head, pool_acc[:, :W], 0.0), M)
    numer = fold_rows(jnp.where(slice_head, pool_acc[:, W:], 0.0), M)
    den = jnp.sum(den_acc[...], axis=0, keepdims=True)
    for p in range(LOW):
        pool_src[p, 0:8, :] = numer[8 * p : 8 * p + 8]
        pool_src[p, 8:16, :] = token_grad[8 * p : 8 * p + 8]
        piece = den[:, (p % 2) * W : (p % 2 + 1) * W]
        pool_src[p, 16:24, :] = jnp.broadcast_to(piece, (8, W))

    pl.semaphore_wait(barrier, parts - 1 + high_n - 1)

    copies = [
        send(pool_src.at[low_peer(k)], pool_recv.at[k - 1], a_send.at[k - 1], a_recv.at[k - 1], low_id(k))
        for k in range(1, LOW)
    ]
    total = pool_src[low]
    for k, copy in enumerate(copies):
        copy.wait()
        total = total + pool_recv[k]
    pool_z[high] = total
    copies = [
        send(pool_z.at[high], pool_z.at[high], b_send.at[k - 1], b_recv.at[k - 1], high_id(k))
        for k in range(1, high_n)
    ]
    for copy in copies:
        copy.wait()
    total = pool_z[0]
    for k in range(1, high_n):
        total = total + pool_z[k]
    pool_full[low] = total
    copies = [
        send(pool_full.at[low], pool_full.at[low], c_send.at[k - 1], c_recv.at[k - 1], low_id(k))
        for k in range(1, LOW)
    ]
    for copy in copies:
        copy.wait()

    numer = jnp.concatenate([pool_full[p, 0:8, :] for p in range(LOW)], axis=0)
    token_grad = jnp.concatenate([pool_full[p, 8:16, :] for p in range(LOW)], axis=0)
    den = jnp.concatenate([pool_full[p, 16:17, :] for p in range(2)], axis=1)
    eye = iota((S, S), 0) == iota((S, S), 1)
    den = jnp.sum(jnp.where(eye, den, 0.0), axis=1, keepdims=True)
    inverse = 1.0 / (den + EPS)
    numer = jnp.where(slice_head, jnp.concatenate([numer] * HEADS, axis=0), 0.0)
    token_grad = jnp.where(slice_head, jnp.concatenate([token_grad] * HEADS, axis=0), 0.0)
    tokens = numer / (den + EPS)
    maps = jnp.concatenate([square_block(r) for r in (wq_ref, wk_ref, wv_ref)], axis=1)
    qkv = dot32(tokens, maps)
    q, k, v = qkv[:, :W], qkv[:, W : 2 * W], qkv[:, 2 * W :]
    inside = iota((S, S), 0) // M == iota((S, S), 1) // M
    scale = 1.0 / math.sqrt(D)
    scores = jnp.where(inside, dot32(q, k, NT) * scale, 0.0)
    e = jnp.where(inside, jnp.exp(scores), 0.0)
    share = e / jnp.sum(e, axis=1, keepdims=True)
    token_out = dot32(share, v).astype(BF16)
    d_share = dot32(token_grad, v, NT)
    d_scores = share * (d_share - jnp.sum(share * d_share, axis=1, keepdims=True)) * scale
    d_qkv = jnp.concatenate(
        [dot32(d_scores, k), dot32(d_scores, q, TN), dot32(share, token_grad, TN)], axis=1
    )
    tok_back = dot32(d_qkv, maps, NT)
    numer_back = (tok_back * inverse).astype(BF16)
    den_back = -jnp.sum(tok_back * tokens, axis=1, keepdims=True) * inverse
    den_back = jnp.sum(jnp.where(eye, den_back, 0.0), axis=0, keepdims=True)
    d_maps = dot32(tokens, d_qkv, TN)
    mix = jnp.concatenate([token_out, numer_back], axis=1)

    xg_acc[...] = jnp.zeros_like(xg_acc)
    slice_acc[...] = jnp.zeros_like(slice_acc)
    proj_acc[...] = jnp.zeros_like(proj_acc)
    bias_acc[...] = jnp.zeros_like(bias_acc)
    temp_acc[...] = jnp.zeros_like(temp_acc)

    def second(i, carry):
        at = pl.ds(pl.multiple_of(i * CHUNK, CHUNK), CHUNK)
        probs = probs_ref[at, :]
        both = dot(pb_ref[at, :], mix)
        mixed = both[:, :W].astype(BF16)
        feat_back = both[:, W:]
        bias_acc[...] += jnp.sum(feat_back.reshape(CHUNK // 8, 8, W), axis=0)
        proj_acc[...] += dot(mixed, g_ref[at, :], TN)
        prob_back = dot(fb_ref[at, :], mix, NT) + den_back
        inner = group_sum(probs * prob_back, ones)
        logit_back = probs * (prob_back - inner)
        temp_acc[...] += jnp.sum((logit_back * logits_ref[at, :]).reshape(CHUNK // 8, 8, S), axis=0)
        score_back = (logit_back * inv_s).astype(BF16)
        mid_back = dot(score_back, a_block, NT).astype(BF16)
        mf = jnp.concatenate([mid_back, feat_back.astype(BF16)], axis=1)
        mf_ref[at, :] = mf
        xg_acc[...] += dot(x_ref[at, :], mf, TN)
        slice_acc[...] += dot(mid_ref[at, :], score_back, TN)
        return carry

    lax.fori_loop(0, rows // CHUNK, second, 0)
    store_mf = pltpu.make_async_copy(mf_ref, mf_hbm, out_sem)
    store_mf.start()

    grad_src[0:W, :] = xg_acc[:, :W]
    grad_src[W : 2 * W, :] = xg_acc[:, W:]
    grad_src[2 * W : 3 * W, :] = proj_acc[...]
    slices = fold_rows(jnp.where(same_head, slice_acc[...], 0.0), D)
    slices = slices[:, :W] + slices[:, W:]
    slices = slices + pltpu.roll(slices, 64, 1)
    slices = slices + pltpu.roll(slices, 32, 1)
    lane = iota((D, W), 1)
    owner = (node == 0).astype(F32)
    block = jnp.where(lane < M, slices, 0.0)
    for i in range(3):
        term = fold_rows(d_maps[:, i * W : (i + 1) * W], D)
        for shift in (64, 32, 16):
            term = term + pltpu.roll(term, shift, 1)
        start = M + i * D
        block = jnp.where((lane >= start) & (lane < start + D), term * owner, block)
    grad_src[3 * W : 3 * W + D, :] = block
    pick_heads = jnp.where(iota((S, W), 0) // M == iota((S, W), 1), 1.0, 0.0)
    temp = jnp.sum(dot32(temp_acc[...] * -inv_s, pick_heads), axis=0, keepdims=True)
    bias = jnp.sum(bias_acc[...], axis=0, keepdims=True)
    row = iota((8, W), 0)
    grad_src[3 * W + D : 3 * W + D + 8, :] = jnp.where(row == 0, bias, jnp.where(row == 1, temp, 0.0))
    used = 3 * W + D + 8
    if used < parts * part_rows:
        grad_src[used:, :] = jnp.zeros((parts * part_rows - used, W), F32)

    def part(ref, p):
        return ref.at[pl.ds(pl.multiple_of(p * part_rows, 8), part_rows), :]

    copies = [
        send(part(grad_src, group_peer(k)), grad_recv.at[k - 1], d_send.at[k - 1], d_recv.at[k - 1], group_id(k))
        for k in range(1, parts)
    ]
    total = part(grad_src, group)[...]
    for k, copy in enumerate(copies):
        copy.wait()
        total = total + grad_recv[k]
    grad_z[high] = total
    copies = [
        send(grad_z.at[high], grad_z.at[high], e_send.at[k - 1], e_recv.at[k - 1], high_id(k))
        for k in range(1, high_n)
    ]
    for copy in copies:
        copy.wait()
    total = grad_z[0]
    for k in range(1, high_n):
        total = total + grad_z[k]
    mine = part(grad_full, group)
    mine[...] = total
    copies = [
        send(mine, mine, f_send.at[k - 1], f_recv.at[k - 1], group_id(k)) for k in range(1, parts)
    ]
    for copy in copies:
        copy.wait()
    packed_ref[...] = grad_full[...]
    store_mf.wait()


def final_kernel(
    packed_ref, mf_ref, w1_ref, w2_ref,
    out_ref, mid_ref, feature_ref, bias_ref, slice_ref, temp_ref, query_ref, key_ref, value_ref, proj_ref,
):
    w12 = jnp.concatenate([w1_ref[...], w2_ref[...]], axis=1)
    out_ref[...] = dot(mf_ref[...], w12, NT)

    @pl.when(pl.program_id(0) == 0)
    def _():
        mid_ref[...] = packed_ref[0:W, :]
        feature_ref[...] = packed_ref[W : 2 * W, :]
        proj_ref[...] = packed_ref[2 * W : 3 * W, :]
        block = packed_ref[3 * W : 3 * W + D, :]
        slice_ref[...] = block[:, 0:M]
        query_ref[...] = block[:, M : M + D]
        key_ref[...] = block[:, M + D : M + 2 * D]
        value_ref[...] = block[:, M + 2 * D : M + 3 * D]
        bias_ref[...] = packed_ref[3 * W + D : 3 * W + D + 1, :]
        temp_ref[...] = packed_ref[3 * W + D + 1 : 3 * W + D + 2, 0:HEADS]


def shards(n_member, n_node, x, g, w1, w2, offset, a, s, wq, wk, wv, w3):
    x, g = x[0], g[0]
    rows = x.shape[0]
    high_n = n_node // LOW
    parts = n_member * LOW
    used = 3 * W + D + 8
    part_rows = -(-used // (8 * parts)) * 8
    vmem = pl.BlockSpec(memory_space=pltpu.VMEM)
    hbm = pl.BlockSpec(memory_space=pl.ANY)
    dma = pltpu.SemaphoreType.DMA
    flops = 2 * rows * S * S * 12
    packed, mf = pl.pallas_call(
        functools.partial(main_kernel, n_member, n_node, parts, part_rows),
        out_shape=(
            jax.ShapeDtypeStruct((parts * part_rows, W), F32),
            jax.ShapeDtypeStruct((rows, 2 * W), BF16),
        ),
        in_specs=[pl.BlockSpec(memory_space=pltpu.SMEM), hbm, hbm] + [vmem] * 8,
        out_specs=(vmem, hbm),
        scratch_shapes=[
            pltpu.VMEM((rows, W), BF16),
            pltpu.VMEM((rows, W), BF16),
            pltpu.VMEM((rows, W), BF16),
            pltpu.VMEM((rows, 2 * W), BF16),
            pltpu.VMEM((rows, S), BF16),
            pltpu.VMEM((rows, S), F32),
            pltpu.VMEM((rows, S), F32),
            pltpu.VMEM((rows, 2 * W), BF16),
            pltpu.VMEM((S, 2 * W), F32),
            pltpu.VMEM((8, S), F32),
            pltpu.VMEM((W, 2 * W), F32),
            pltpu.VMEM((W, S), F32),
            pltpu.VMEM((W, W), F32),
            pltpu.VMEM((8, W), F32),
            pltpu.VMEM((8, S), F32),
            pltpu.VMEM((LOW, 24, W), F32),
            pltpu.VMEM((LOW - 1, 24, W), F32),
            pltpu.VMEM((high_n, 24, W), F32),
            pltpu.VMEM((LOW, 24, W), F32),
            pltpu.VMEM((parts * part_rows, W), F32),
            pltpu.VMEM((parts - 1, part_rows, W), F32),
            pltpu.VMEM((high_n, part_rows, W), F32),
            pltpu.VMEM((parts * part_rows, W), F32),
            dma((2,)),
            dma,
            dma((LOW - 1,)), dma((LOW - 1,)),
            dma((high_n - 1,)), dma((high_n - 1,)),
            dma((LOW - 1,)), dma((LOW - 1,)),
            dma((parts - 1,)), dma((parts - 1,)),
            dma((high_n - 1,)), dma((high_n - 1,)),
            dma((parts - 1,)), dma((parts - 1,)),
        ],
        compiler_params=pltpu.CompilerParams(
            collective_id=0, has_side_effects=True, vmem_limit_bytes=48 * 1024 * 1024
        ),
        cost_estimate=pl.CostEstimate(
            flops=flops, bytes_accessed=rows * W * 8, transcendentals=rows * S
        ),
        name="pool_and_gradients",
    )(s, x, g, w1, w2, offset.reshape(1, W), a, wq, wk, wv, w3)

    tile = 1024
    whole = lambda *shape: pl.BlockSpec(shape, lambda i: (0,) * len(shape))
    outs = pl.pallas_call(
        final_kernel,
        grid=(rows // tile,),
        out_shape=(
            jax.ShapeDtypeStruct((rows, W), F32),
            jax.ShapeDtypeStruct((W, W), F32),
            jax.ShapeDtypeStruct((W, W), F32),
            jax.ShapeDtypeStruct((1, W), F32),
            jax.ShapeDtypeStruct((D, M), F32),
            jax.ShapeDtypeStruct((1, HEADS), F32),
            jax.ShapeDtypeStruct((D, D), F32),
            jax.ShapeDtypeStruct((D, D), F32),
            jax.ShapeDtypeStruct((D, D), F32),
            jax.ShapeDtypeStruct((W, W), F32),
        ),
        in_specs=[
            whole(parts * part_rows, W),
            pl.BlockSpec((tile, 2 * W), lambda i: (i, 0)),
            whole(W, W),
            whole(W, W),
        ],
        out_specs=(
            pl.BlockSpec((tile, W), lambda i: (i, 0)),
            whole(W, W), whole(W, W), whole(1, W), whole(D, M), whole(1, HEADS),
            whole(D, D), whole(D, D), whole(D, D), whole(W, W),
        ),
        compiler_params=pltpu.CompilerParams(vmem_limit_bytes=32 * 1024 * 1024),
        cost_estimate=pl.CostEstimate(
            flops=2 * rows * 2 * W * W, bytes_accessed=rows * W * 8, transcendentals=0
        ),
        name="vertex_and_unpack",
    )(packed, mf, w1, w2)
    vertex, mid, feature, bias, slices, temp, query, key, value, proj = outs
    return (
        vertex[None], mid, feature, bias.reshape(W), slices, temp.reshape(HEADS),
        query, key, value, proj,
    )


def solution(mesh):
    spread = P("member", "node", None)
    return jax.shard_map(
        functools.partial(shards, mesh.shape["member"], mesh.shape["node"]),
        mesh=mesh,
        in_specs=(spread, spread) + (P(),) * 9,
        out_specs=(spread,) + (P(),) * 9,
        check_vma=False,
    )
```

```python
import functools
import math

import jax
import jax.numpy as jnp
from jax import lax
from jax.experimental import pallas as pl
from jax.experimental.pallas import tpu as pltpu
from jax.sharding import PartitionSpec as P

W = 128
HEADS = 8
M = 32
D = 16
S = HEADS * M
LOW = 4
CHUNK = 512
EPS = 1e-05
VMEM_LIMIT = 62 * 1024 * 1024
F32 = jnp.float32
BF16 = jnp.bfloat16
MESH = pl.DeviceIdType.MESH

NN = (((1,), (0,)), ((), ()))
NT = (((1,), (1,)), ((), ()))
TN = (((0,), (0,)), ((), ()))


def dot(a, b, dims=NN):
    return lax.dot_general(a, b, dims, preferred_element_type=F32)


def split(a):
    upper = a.astype(BF16)
    return upper, (a - upper.astype(F32)).astype(BF16)


def dot32(a, b, dims=NN):
    a_parts = (a,) if a.dtype == BF16 else split(a)
    b_parts = (b,) if b.dtype == BF16 else split(b)
    total = dot(a_parts[0], b_parts[0], dims)
    if len(b_parts) == 2:
        total = total + dot(a_parts[0], b_parts[1], dims)
    if len(a_parts) == 2:
        total = total + dot(a_parts[1], b_parts[0], dims)
    return total


def iota(shape, axis):
    return lax.broadcasted_iota(jnp.int32, shape, axis)


def group_sum(values, ones):
    return dot32(values, ones)


def fold_rows(a, step):
    total = a[0:step]
    for i in range(step, a.shape[0], step):
        total = total + a[i : i + step]
    return total


def main_kernel(
    n_member, n_node, parts, early_rows, late_rows,
    s_ref, x_hbm, g_hbm, w1_ref, w2_ref, off_ref, a_ref, wq_ref, wk_ref, wv_ref, w3_ref,
    packed_ref, mf_hbm,
    x_ref, g_ref, mid_ref, fb_ref, pb_ref, probs_ref, logits_ref, mf_ref,
    xt_ref, gt_ref, midt_ref,
    pool_acc, den_acc, mid_acc, feature_acc, slice_acc, proj_acc, bias_acc, temp_acc,
    pool_src, pool_recv, pool_z, pool_full,
    early_src, early_recv, early_z, early_full, late_src, late_recv, late_z, late_full,
    in_sem, out_sem,
    a_send, a_recv, b_send, b_recv, c_send, c_recv,
    early_sems, late_sems,
):
    rows = x_ref.shape[0]
    high_n = n_node // LOW
    member, node = lax.axis_index("member"), lax.axis_index("node")
    low, high = lax.rem(node, LOW), lax.div(node, LOW)
    group = member * LOW + low

    def low_peer(k):
        return lax.rem(low + k, LOW)

    def high_peer(k):
        return lax.rem(high + k, high_n)

    def group_peer(k):
        return lax.rem(group + k, parts)

    def low_id(k):
        return (member, high * LOW + low_peer(k))

    def high_id(k):
        return (member, high_peer(k) * LOW + low)

    def group_id(k):
        peer = group_peer(k)
        return (lax.div(peer, LOW), high * LOW + lax.rem(peer, LOW))

    load_x = pltpu.make_async_copy(x_hbm, x_ref, in_sem.at[0])
    load_g = pltpu.make_async_copy(g_hbm, g_ref, in_sem.at[1])
    load_x.start()
    load_g.start()

    barrier = pltpu.get_barrier_semaphore()
    for k in range(1, parts):
        pl.semaphore_signal(barrier, inc=1, device_id=group_id(k), device_id_type=MESH)
    for k in range(1, high_n):
        pl.semaphore_signal(barrier, inc=1, device_id=high_id(k), device_id_type=MESH)

    def send(src, dst, send_sem, recv_sem, target):
        copy = pltpu.make_async_remote_copy(
            src_ref=src, dst_ref=dst, send_sem=send_sem, recv_sem=recv_sem,
            device_id=target, device_id_type=MESH,
        )
        copy.start()
        return copy

    head_of_slice = iota((1, S), 1) // M
    inv_s = jnp.zeros((1, S), F32)
    for h in range(HEADS):
        inv_s = jnp.where(head_of_slice == h, 1.0 / jnp.full((1, S), s_ref[h], F32), inv_s)
    ones = jnp.where(iota((S, S), 0) // M == iota((S, S), 1) // M, 1.0, 0.0).astype(BF16)
    same_head = iota((W, S), 0) // D == iota((W, S), 1) // M
    pick_rows = jnp.where(iota((W, D), 0) % D == iota((W, D), 1), 1.0, 0.0).astype(BF16)
    pick_slices = jnp.where(iota((M, S), 1) % M == iota((M, S), 0), 1.0, 0.0).astype(BF16)
    pick_columns = jnp.where(iota((D, W), 1) % D == iota((D, W), 0), 1.0, 0.0).astype(BF16)
    a_all = dot(dot(pick_rows, a_ref[...]).astype(BF16), pick_slices)
    a_block = jnp.where(same_head, a_all, 0.0).astype(BF16)
    head_square = iota((W, W), 0) // D == iota((W, W), 1) // D

    def square_block(ref):
        return jnp.where(
            head_square, dot(dot(pick_rows, ref[...]).astype(BF16), pick_columns), 0.0
        ).astype(BF16)

    w12 = jnp.concatenate([w1_ref[...], w2_ref[...]], axis=1)
    w3 = w3_ref[...]
    offset = off_ref[...]

    pool_acc[...] = jnp.zeros_like(pool_acc)
    den_acc[...] = jnp.zeros_like(den_acc)
    load_x.wait()
    load_g.wait()

    def first(i, carry):
        at = pl.ds(pl.multiple_of(i * CHUNK, CHUNK), CHUNK)
        x = x_ref[at, :]
        both = dot(x, w12)
        mid = both[:, :W].astype(BF16)
        feat = (both[:, W:] + offset).astype(BF16)
        back = dot(g_ref[at, :], w3, NT).astype(BF16)
        logits = dot(mid, a_block) * inv_s
        e = jnp.exp(logits)
        probs = e / group_sum(e, ones)
        pb = probs.astype(BF16)
        fb = jnp.concatenate([back, feat], axis=1)
        mid_ref[at, :] = mid
        fb_ref[at, :] = fb
        pb_ref[at, :] = pb
        probs_ref[at, :] = probs
        logits_ref[at, :] = logits
        pool_acc[...] += dot(pb, fb, TN)
        den_acc[...] += jnp.sum(probs.reshape(CHUNK // 8, 8, S), axis=0)
        return carry

    lax.fori_loop(0, rows // CHUNK, first, 0)

    slice_head = iota((S, W), 0) // M == iota((S, W), 1) // D
    token_grad = fold_rows(jnp.where(slice_head, pool_acc[:, :W], 0.0), M)
    numer = fold_rows(jnp.where(slice_head, pool_acc[:, W:], 0.0), M)
    den = jnp.sum(den_acc[...], axis=0, keepdims=True)
    for p in range(LOW):
        pool_src[p, 0:8, :] = numer[8 * p : 8 * p + 8]
        pool_src[p, 8:16, :] = token_grad[8 * p : 8 * p + 8]
        piece = den[:, (p % 2) * W : (p % 2 + 1) * W]
        pool_src[p, 16:24, :] = jnp.broadcast_to(piece, (8, W))

    pl.semaphore_wait(barrier, parts - 1 + high_n - 1)

    copies = [
        send(pool_src.at[low_peer(k)], pool_recv.at[k - 1], a_send.at[k - 1], a_recv.at[k - 1], low_id(k))
        for k in range(1, LOW)
    ]
    def turn(source, target):
        def step(i, carry):
            at = pl.ds(pl.multiple_of(i * CHUNK, CHUNK), CHUNK)
            target[i] = source[at, :].T
            return carry

        lax.fori_loop(0, rows // CHUNK, step, 0)

    turn(x_ref, xt_ref)
    total = pool_src[low]
    for k, copy in enumerate(copies):
        copy.wait()
        total = total + pool_recv[k]
    pool_z[high] = total
    copies = [
        send(pool_z.at[high], pool_z.at[high], b_send.at[k - 1], b_recv.at[k - 1], high_id(k))
        for k in range(1, high_n)
    ]
    turn(g_ref, gt_ref)
    turn(mid_ref, midt_ref)
    for copy in copies:
        copy.wait()
    total = pool_z[0]
    for k in range(1, high_n):
        total = total + pool_z[k]
    pool_full[low] = total
    copies = [
        send(pool_full.at[low], pool_full.at[low], c_send.at[k - 1], c_recv.at[k - 1], low_id(k))
        for k in range(1, LOW)
    ]
    for copy in copies:
        copy.wait()

    numer = jnp.concatenate([pool_full[p, 0:8, :] for p in range(LOW)], axis=0)
    token_grad = jnp.concatenate([pool_full[p, 8:16, :] for p in range(LOW)], axis=0)
    den = jnp.concatenate([pool_full[p, 16:17, :] for p in range(2)], axis=1)
    eye = iota((S, S), 0) == iota((S, S), 1)
    den = jnp.sum(jnp.where(eye, den, 0.0), axis=1, keepdims=True)
    inverse = 1.0 / (den + EPS)
    numer = jnp.where(slice_head, jnp.concatenate([numer] * HEADS, axis=0), 0.0)
    token_grad = jnp.where(slice_head, jnp.concatenate([token_grad] * HEADS, axis=0), 0.0)
    tokens = numer / (den + EPS)
    maps = jnp.concatenate([square_block(r) for r in (wq_ref, wk_ref, wv_ref)], axis=1)
    qkv = dot32(tokens, maps)
    q, k, v = qkv[:, :W], qkv[:, W : 2 * W], qkv[:, 2 * W :]
    inside = iota((S, S), 0) // M == iota((S, S), 1) // M
    scale = 1.0 / math.sqrt(D)
    scores = jnp.where(inside, dot32(q, k, NT) * scale, 0.0)
    e = jnp.where(inside, jnp.exp(scores), 0.0)
    share = e / jnp.sum(e, axis=1, keepdims=True)
    token_out = dot32(share, v).astype(BF16)
    d_share = dot32(token_grad, v, NT)
    d_scores = share * (d_share - jnp.sum(share * d_share, axis=1, keepdims=True)) * scale
    d_qkv = jnp.concatenate(
        [dot32(d_scores, k), dot32(d_scores, q, TN), dot32(share, token_grad, TN)], axis=1
    )
    tok_back = dot32(d_qkv, maps, NT)
    numer_back = (tok_back * inverse).astype(BF16)
    den_back = -jnp.sum(tok_back * tokens, axis=1, keepdims=True) * inverse
    den_back = jnp.sum(jnp.where(eye, den_back, 0.0), axis=0, keepdims=True)
    d_maps = dot32(tokens, d_qkv, TN)
    mix = jnp.concatenate([token_out, numer_back], axis=1)

    for acc in (mid_acc, feature_acc, slice_acc, proj_acc, bias_acc, temp_acc):
        acc[...] = jnp.zeros_like(acc)

    def part(ref, p, size):
        return ref.at[pl.ds(pl.multiple_of(p * size, 8), size), :]

    def start_scatter(src, recv, size, sems):
        return [
            send(part(src, group_peer(k), size), recv.at[k - 1], sems.at[0, k - 1], sems.at[1, k - 1], group_id(k))
            for k in range(1, parts)
        ]

    def start_across(copies, src, recv, z, size, sems):
        total = part(src, group, size)[...]
        for k, copy in enumerate(copies):
            copy.wait()
            total = total + recv[k]
        z[high] = total
        return [
            send(z.at[high], z.at[high], sems.at[2, k - 1], sems.at[3, k - 1], high_id(k))
            for k in range(1, high_n)
        ]

    def start_gather(copies, z, full, size, sems):
        for copy in copies:
            copy.wait()
        total = z[0]
        for k in range(1, high_n):
            total = total + z[k]
        mine = part(full, group, size)
        mine[...] = total
        return [
            send(mine, mine, sems.at[4, k - 1], sems.at[5, k - 1], group_id(k))
            for k in range(1, parts)
        ]

    def second(i, carry):
        at = pl.ds(pl.multiple_of(i * CHUNK, CHUNK), CHUNK)
        both = dot(pb_ref[at, :], mix)
        mixed = both[:, :W].astype(BF16)
        feat_back = both[:, W:]
        rounded = feat_back.astype(BF16)
        mf_ref[at, W:] = rounded
        bias_acc[...] += jnp.sum(feat_back.reshape(CHUNK // 8, 8, W), axis=0)
        proj_acc[...] += dot(gt_ref[i], mixed)
        feature_acc[...] += dot(xt_ref[i], rounded)
        return carry

    def third(i, carry):
        at = pl.ds(pl.multiple_of(i * CHUNK, CHUNK), CHUNK)
        probs = probs_ref[at, :]
        prob_back = dot(fb_ref[at, :], mix, NT) + den_back
        inner = group_sum(probs * prob_back, ones)
        logit_back = probs * (prob_back - inner)
        temp_acc[...] += jnp.sum((logit_back * logits_ref[at, :]).reshape(CHUNK // 8, 8, S), axis=0)
        score_back = (logit_back * inv_s).astype(BF16)
        mid_back = dot(score_back, a_block, NT).astype(BF16)
        mf_ref[at, :W] = mid_back
        mid_acc[...] += dot(xt_ref[i], mid_back)
        slice_acc[...] += dot(midt_ref[i], score_back)
        return carry

    steps = rows // CHUNK
    lax.fori_loop(0, steps, second, 0)
    early_src[0:W, :] = feature_acc[...]
    early_src[W : 2 * W, :] = proj_acc[...].T
    early = start_scatter(early_src, early_recv, early_rows, early_sems)
    lax.fori_loop(0, steps // 2, third, 0)
    early = start_across(early, early_src, early_recv, early_z, early_rows, early_sems)
    lax.fori_loop(steps // 2, steps, third, 0)
    store_mf = pltpu.make_async_copy(mf_ref, mf_hbm, out_sem)
    store_mf.start()
    early = start_gather(early, early_z, early_full, early_rows, early_sems)

    late_src[0:W, :] = mid_acc[...]
    slices = fold_rows(jnp.where(same_head, slice_acc[...], 0.0), D)
    slices = slices[:, :W] + slices[:, W:]
    slices = slices + pltpu.roll(slices, 64, 1)
    slices = slices + pltpu.roll(slices, 32, 1)
    lane = iota((D, W), 1)
    owner = (node == 0).astype(F32)
    block = jnp.where(lane < M, slices, 0.0)
    for i in range(3):
        term = fold_rows(d_maps[:, i * W : (i + 1) * W], D)
        for shift in (64, 32, 16):
            term = term + pltpu.roll(term, shift, 1)
        start = M + i * D
        block = jnp.where((lane >= start) & (lane < start + D), term * owner, block)
    late_src[W : W + D, :] = block
    pick_heads = jnp.where(iota((S, W), 0) // M == iota((S, W), 1), 1.0, 0.0).astype(BF16)
    temp = jnp.sum(dot32(temp_acc[...] * -inv_s, pick_heads), axis=0, keepdims=True)
    bias = jnp.sum(bias_acc[...], axis=0, keepdims=True)
    row = iota((8, W), 0)
    late_src[W + D : W + D + 8, :] = jnp.where(row == 0, bias, jnp.where(row == 1, temp, 0.0))
    used = W + D + 8
    if used < parts * late_rows:
        late_src[used:, :] = jnp.zeros((parts * late_rows - used, W), F32)

    late = start_scatter(late_src, late_recv, late_rows, late_sems)
    late = start_across(late, late_src, late_recv, late_z, late_rows, late_sems)
    late = start_gather(late, late_z, late_full, late_rows, late_sems)
    for copy in early:
        copy.wait()
    packed_ref[0 : 2 * W, :] = early_full[...]
    for copy in late:
        copy.wait()
    packed_ref[2 * W :, :] = late_full[...]
    store_mf.wait()


def final_kernel(
    packed_ref, mf_ref, w1_ref, w2_ref,
    out_ref, mid_ref, feature_ref, bias_ref, slice_ref, temp_ref, query_ref, key_ref, value_ref, proj_ref,
):
    w12 = jnp.concatenate([w1_ref[...], w2_ref[...]], axis=1)
    out_ref[...] = dot(mf_ref[...], w12, NT)

    @pl.when(pl.program_id(0) == 0)
    def _():
        feature_ref[...] = packed_ref[0:W, :]
        proj_ref[...] = packed_ref[W : 2 * W, :]
        mid_ref[...] = packed_ref[2 * W : 3 * W, :]
        block = packed_ref[3 * W : 3 * W + D, :]
        slice_ref[...] = block[:, 0:M]
        query_ref[...] = block[:, M : M + D]
        key_ref[...] = block[:, M + D : M + 2 * D]
        value_ref[...] = block[:, M + 2 * D : M + 3 * D]
        bias_ref[...] = packed_ref[3 * W + D : 3 * W + D + 1, :]
        temp_ref[...] = packed_ref[3 * W + D + 1 : 3 * W + D + 2, 0:HEADS]


def shards(n_member, n_node, x, g, w1, w2, offset, a, s, wq, wk, wv, w3):
    x, g = x[0], g[0]
    rows = x.shape[0]
    high_n = n_node // LOW
    parts = n_member * LOW
    early_rows = -(-2 * W // (8 * parts)) * 8
    late_rows = -(-(W + D + 8) // (8 * parts)) * 8
    packed_rows = 2 * W + parts * late_rows
    assert parts * early_rows == 2 * W and n_node % LOW == 0
    vmem = pl.BlockSpec(memory_space=pltpu.VMEM)
    hbm = pl.BlockSpec(memory_space=pl.ANY)
    dma = pltpu.SemaphoreType.DMA
    flops = 2 * rows * S * S * 12
    packed, mf = pl.pallas_call(
        functools.partial(main_kernel, n_member, n_node, parts, early_rows, late_rows),
        out_shape=(
            jax.ShapeDtypeStruct((packed_rows, W), F32),
            jax.ShapeDtypeStruct((rows, 2 * W), BF16),
        ),
        in_specs=[pl.BlockSpec(memory_space=pltpu.SMEM), hbm, hbm] + [vmem] * 8,
        out_specs=(vmem, hbm),
        scratch_shapes=[
            pltpu.VMEM((rows, W), BF16),
            pltpu.VMEM((rows, W), BF16),
            pltpu.VMEM((rows, W), BF16),
            pltpu.VMEM((rows, 2 * W), BF16),
            pltpu.VMEM((rows, S), BF16),
            pltpu.VMEM((rows, S), F32),
            pltpu.VMEM((rows, S), F32),
            pltpu.VMEM((rows, 2 * W), BF16),
            pltpu.VMEM((rows // CHUNK, W, CHUNK), BF16),
            pltpu.VMEM((rows // CHUNK, W, CHUNK), BF16),
            pltpu.VMEM((rows // CHUNK, W, CHUNK), BF16),
            pltpu.VMEM((S, 2 * W), F32),
            pltpu.VMEM((8, S), F32),
            pltpu.VMEM((W, W), F32),
            pltpu.VMEM((W, W), F32),
            pltpu.VMEM((W, S), F32),
            pltpu.VMEM((W, W), F32),
            pltpu.VMEM((8, W), F32),
            pltpu.VMEM((8, S), F32),
            pltpu.VMEM((LOW, 24, W), F32),
            pltpu.VMEM((LOW - 1, 24, W), F32),
            pltpu.VMEM((high_n, 24, W), F32),
            pltpu.VMEM((LOW, 24, W), F32),
            pltpu.VMEM((parts * early_rows, W), F32),
            pltpu.VMEM((parts - 1, early_rows, W), F32),
            pltpu.VMEM((high_n, early_rows, W), F32),
            pltpu.VMEM((parts * early_rows, W), F32),
            pltpu.VMEM((parts * late_rows, W), F32),
            pltpu.VMEM((parts - 1, late_rows, W), F32),
            pltpu.VMEM((high_n, late_rows, W), F32),
            pltpu.VMEM((parts * late_rows, W), F32),
            dma((2,)),
            dma,
            dma((LOW - 1,)), dma((LOW - 1,)),
            dma((high_n - 1,)), dma((high_n - 1,)),
            dma((LOW - 1,)), dma((LOW - 1,)),
            dma((6, max(parts, high_n) - 1)),
            dma((6, max(parts, high_n) - 1)),
        ],
        compiler_params=pltpu.CompilerParams(
            collective_id=0, has_side_effects=True, vmem_limit_bytes=VMEM_LIMIT
        ),
        cost_estimate=pl.CostEstimate(
            flops=flops, bytes_accessed=rows * W * 8, transcendentals=rows * S
        ),
        name="pool_and_gradients",
    )(s, x, g, w1, w2, offset.reshape(1, W), a, wq, wk, wv, w3)

    tile = 1024
    whole = lambda *shape: pl.BlockSpec(shape, lambda i: (0,) * len(shape))
    outs = pl.pallas_call(
        final_kernel,
        grid=(rows // tile,),
        out_shape=(
            jax.ShapeDtypeStruct((rows, W), F32),
            jax.ShapeDtypeStruct((W, W), F32),
            jax.ShapeDtypeStruct((W, W), F32),
            jax.ShapeDtypeStruct((1, W), F32),
            jax.ShapeDtypeStruct((D, M), F32),
            jax.ShapeDtypeStruct((1, HEADS), F32),
            jax.ShapeDtypeStruct((D, D), F32),
            jax.ShapeDtypeStruct((D, D), F32),
            jax.ShapeDtypeStruct((D, D), F32),
            jax.ShapeDtypeStruct((W, W), F32),
        ),
        in_specs=[
            whole(packed_rows, W),
            pl.BlockSpec((tile, 2 * W), lambda i: (i, 0)),
            whole(W, W),
            whole(W, W),
        ],
        out_specs=(
            pl.BlockSpec((tile, W), lambda i: (i, 0)),
            whole(W, W), whole(W, W), whole(1, W), whole(D, M), whole(1, HEADS),
            whole(D, D), whole(D, D), whole(D, D), whole(W, W),
        ),
        compiler_params=pltpu.CompilerParams(vmem_limit_bytes=VMEM_LIMIT),
        cost_estimate=pl.CostEstimate(
            flops=2 * rows * 2 * W * W, bytes_accessed=rows * W * 8, transcendentals=0
        ),
        name="vertex_and_unpack",
    )(packed, mf, w1, w2)
    vertex, mid, feature, bias, slices, temp, query, key, value, proj = outs
    return (
        vertex[None], mid, feature, bias.reshape(W), slices, temp.reshape(HEADS),
        query, key, value, proj,
    )


def solution(mesh):
    spread = P("member", "node", None)
    return jax.shard_map(
        functools.partial(shards, mesh.shape["member"], mesh.shape["node"]),
        mesh=mesh,
        in_specs=(spread, spread) + (P(),) * 9,
        out_specs=(spread,) + (P(),) * 9,
        check_vma=False,
    )
```

```python
import functools
import math

import jax
import jax.numpy as jnp
from jax import lax
from jax.experimental import pallas as pl
from jax.experimental.pallas import tpu as pltpu
from jax.sharding import PartitionSpec as P

W = 128
HEADS = 8
M = 32
D = 16
S = HEADS * M
LOW = 4
CHUNK = 1024
EPS = 1e-05
PIECES = 4
VMEM_LIMIT = 62 * 1024 * 1024
F32 = jnp.float32
BF16 = jnp.bfloat16
MESH = pl.DeviceIdType.MESH

NN = (((1,), (0,)), ((), ()))
NT = (((1,), (1,)), ((), ()))
TN = (((0,), (0,)), ((), ()))


def dot(a, b, dims=NN):
    return lax.dot_general(a, b, dims, preferred_element_type=F32)


def split(a):
    upper = a.astype(BF16)
    return upper, (a - upper.astype(F32)).astype(BF16)


def dot32(a, b, dims=NN):
    a_parts = (a,) if a.dtype == BF16 else split(a)
    b_parts = (b,) if b.dtype == BF16 else split(b)
    total = dot(a_parts[0], b_parts[0], dims)
    if len(b_parts) == 2:
        total = total + dot(a_parts[0], b_parts[1], dims)
    if len(a_parts) == 2:
        total = total + dot(a_parts[1], b_parts[0], dims)
    return total


def iota(shape, axis):
    return lax.broadcasted_iota(jnp.int32, shape, axis)


def block_of(index, size):
    return index >> (size.bit_length() - 1)


def group_sum(values, ones):
    return dot(jnp.concatenate(split(values), axis=1), ones)


def fold_rows(a, step):
    total = a[0:step]
    for i in range(step, a.shape[0], step):
        total = total + a[i : i + step]
    return total


def main_kernel(
    n_member, n_node, parts, early_rows, late_rows,
    s_ref, x_hbm, g_hbm, w1_ref, w2_ref, off_ref, a_ref, wq_ref, wk_ref, wv_ref, w3_ref,
    packed_ref, vertex_hbm,
    x_ref, g_ref, mid_ref, fb_ref, pb_ref, probs_ref, logits_ref, mf_ref, vertex_ref,
    xt_ref, gt_ref, midt_ref,
    pool_acc, den_acc, mid_acc, feature_acc, slice_acc, proj_acc, bias_acc, temp_acc,
    pool_src, pool_recv, pool_z, pool_full,
    early_src, early_recv, early_z, early_full, late_src, late_recv, late_z, late_full,
    in_sem, out_sem,
    a_send, a_recv, b_send, b_recv, c_send, c_recv,
    early_sems, late_sems,
):
    rows = x_ref.shape[0]
    high_n = n_node // LOW
    member, node = lax.axis_index("member"), lax.axis_index("node")
    low, high = lax.rem(node, LOW), lax.div(node, LOW)
    group = member * LOW + low

    def low_peer(k):
        return lax.rem(low + k, LOW)

    def high_peer(k):
        return lax.rem(high + k, high_n)

    def group_peer(k):
        return lax.rem(group + k, parts)

    def low_id(k):
        return (member, high * LOW + low_peer(k))

    def high_id(k):
        return (member, high_peer(k) * LOW + low)

    def group_id(k):
        peer = group_peer(k)
        return (lax.div(peer, LOW), high * LOW + lax.rem(peer, LOW))

    def load(i):
        at = pl.ds(pl.multiple_of(i * CHUNK, CHUNK), CHUNK)
        return (
            pltpu.make_async_copy(x_hbm.at[at, :], x_ref.at[at, :], in_sem.at[0, i]),
            pltpu.make_async_copy(g_hbm.at[at, :], g_ref.at[at, :], in_sem.at[1, i]),
        )

    for i in range(rows // CHUNK):
        for copy in load(i):
            copy.start()

    barrier = pltpu.get_barrier_semaphore()
    for k in range(1, parts):
        pl.semaphore_signal(barrier, inc=1, device_id=group_id(k), device_id_type=MESH)
    for k in range(1, high_n):
        pl.semaphore_signal(barrier, inc=1, device_id=high_id(k), device_id_type=MESH)

    def send(src, dst, send_sem, recv_sem, target):
        copy = pltpu.make_async_remote_copy(
            src_ref=src, dst_ref=dst, send_sem=send_sem, recv_sem=recv_sem,
            device_id=target, device_id_type=MESH,
        )
        copy.start()
        return copy

    head_of_slice = block_of(iota((1, S), 1), M)
    inv_s = jnp.zeros((1, S), F32)
    for h in range(HEADS):
        inv_s = jnp.where(head_of_slice == h, 1.0 / jnp.full((1, S), s_ref[h], F32), inv_s)
    inside = block_of(iota((S, S), 0), M) == block_of(iota((S, S), 1), M)
    ones = jnp.where(inside, 1.0, 0.0).astype(BF16)
    ones = jnp.concatenate([ones, ones], axis=0)
    same_head = block_of(iota((W, S), 0), D) == block_of(iota((W, S), 1), M)
    pick_rows = jnp.where((iota((W, D), 0) & (D - 1)) == iota((W, D), 1), 1.0, 0.0).astype(BF16)
    pick_slices = jnp.where((iota((M, S), 1) & (M - 1)) == iota((M, S), 0), 1.0, 0.0).astype(BF16)
    pick_columns = jnp.where((iota((D, W), 1) & (D - 1)) == iota((D, W), 0), 1.0, 0.0).astype(BF16)
    a_all = dot(dot(pick_rows, a_ref[...]).astype(BF16), pick_slices)
    a_block = jnp.where(same_head, a_all, 0.0).astype(BF16)
    head_square = block_of(iota((W, W), 0), D) == block_of(iota((W, W), 1), D)

    def square_block(ref):
        return jnp.where(
            head_square, dot(dot(pick_rows, ref[...]).astype(BF16), pick_columns), 0.0
        ).astype(BF16)

    w12 = jnp.concatenate([w1_ref[...], w2_ref[...]], axis=1)
    w3 = w3_ref[...]
    offset = off_ref[...]

    pool_acc[...] = jnp.zeros_like(pool_acc)
    den_acc[...] = jnp.zeros_like(den_acc)

    def first(i, carry):
        for copy in load(i):
            copy.wait()
        at = pl.ds(pl.multiple_of(i * CHUNK, CHUNK), CHUNK)
        x = x_ref[at, :]
        both = dot(x, w12)
        mid = both[:, :W].astype(BF16)
        feat = (both[:, W:] + offset).astype(BF16)
        back = dot(g_ref[at, :], w3, NT).astype(BF16)
        logits = dot(mid, a_block) * inv_s
        e = jnp.exp(logits)
        total = group_sum(e, ones)
        guess = pl.reciprocal(total, approx=True)
        probs = e * (guess * (2.0 - total * guess))
        pb = probs.astype(BF16)
        fb = jnp.concatenate([back, feat], axis=1)
        mid_ref[at, :] = mid
        fb_ref[at, :] = fb
        pb_ref[at, :] = pb
        probs_ref[at, :] = probs
        logits_ref[at, :] = logits
        pool_acc[...] += dot(pb, fb, TN)
        den_acc[...] += jnp.sum(probs.reshape(CHUNK // 8, 8, S), axis=0)
        return carry

    lax.fori_loop(0, rows // CHUNK, first, 0)

    slice_head = block_of(iota((S, W), 0), M) == block_of(iota((S, W), 1), D)
    token_grad = fold_rows(jnp.where(slice_head, pool_acc[:, :W], 0.0), M)
    numer = fold_rows(jnp.where(slice_head, pool_acc[:, W:], 0.0), M)
    den = jnp.sum(den_acc[...], axis=0, keepdims=True)
    for p in range(LOW):
        pool_src[p, 0:8, :] = numer[8 * p : 8 * p + 8]
        pool_src[p, 8:16, :] = token_grad[8 * p : 8 * p + 8]
        piece = den[:, (p % 2) * W : (p % 2 + 1) * W]
        pool_src[p, 16:24, :] = jnp.broadcast_to(piece, (8, W))

    pl.semaphore_wait(barrier, parts - 1 + high_n - 1)

    copies = [
        send(pool_src.at[low_peer(k)], pool_recv.at[k - 1], a_send.at[k - 1], a_recv.at[k - 1], low_id(k))
        for k in range(1, LOW)
    ]
    def turn(source, target):
        def step(i, carry):
            at = pl.ds(pl.multiple_of(i * CHUNK, CHUNK), CHUNK)
            target[i] = source[at, :].T
            return carry

        lax.fori_loop(0, rows // CHUNK, step, 0)

    turn(x_ref, xt_ref)
    total = pool_src[low]
    for k, copy in enumerate(copies):
        copy.wait()
        total = total + pool_recv[k]
    pool_z[high] = total
    copies = [
        send(pool_z.at[high], pool_z.at[high], b_send.at[k - 1], b_recv.at[k - 1], high_id(k))
        for k in range(1, high_n)
    ]
    turn(g_ref, gt_ref)
    turn(mid_ref, midt_ref)
    for copy in copies:
        copy.wait()
    total = pool_z[0]
    for k in range(1, high_n):
        total = total + pool_z[k]
    pool_full[low] = total
    copies = [
        send(pool_full.at[low], pool_full.at[low], c_send.at[k - 1], c_recv.at[k - 1], low_id(k))
        for k in range(1, LOW)
    ]
    for copy in copies:
        copy.wait()

    numer = jnp.concatenate([pool_full[p, 0:8, :] for p in range(LOW)], axis=0)
    token_grad = jnp.concatenate([pool_full[p, 8:16, :] for p in range(LOW)], axis=0)
    den = jnp.concatenate([pool_full[p, 16:17, :] for p in range(2)], axis=1)
    eye = iota((S, S), 0) == iota((S, S), 1)
    den = jnp.sum(jnp.where(eye, den, 0.0), axis=1, keepdims=True)
    inverse = 1.0 / (den + EPS)
    numer = jnp.where(slice_head, jnp.concatenate([numer] * HEADS, axis=0), 0.0)
    token_grad = jnp.where(slice_head, jnp.concatenate([token_grad] * HEADS, axis=0), 0.0)
    tokens = numer / (den + EPS)
    maps = jnp.concatenate([square_block(r) for r in (wq_ref, wk_ref, wv_ref)], axis=1)
    qkv = dot32(tokens, maps)
    q, k, v = qkv[:, :W], qkv[:, W : 2 * W], qkv[:, 2 * W :]
    scale = 1.0 / math.sqrt(D)
    scores = jnp.where(inside, dot32(q, k, NT) * scale, 0.0)
    e = jnp.where(inside, jnp.exp(scores), 0.0)
    share = e / jnp.sum(e, axis=1, keepdims=True)
    token_out = dot32(share, v).astype(BF16)
    d_share = dot32(token_grad, v, NT)
    d_scores = share * (d_share - jnp.sum(share * d_share, axis=1, keepdims=True)) * scale
    d_qkv = jnp.concatenate(
        [dot32(d_scores, k), dot32(d_scores, q, TN), dot32(share, token_grad, TN)], axis=1
    )
    tok_back = dot32(d_qkv, maps, NT)
    numer_back = (tok_back * inverse).astype(BF16)
    den_back = -jnp.sum(tok_back * tokens, axis=1, keepdims=True) * inverse
    den_back = jnp.sum(jnp.where(eye, den_back, 0.0), axis=0, keepdims=True)
    d_maps = dot32(tokens, d_qkv, TN)
    mix = jnp.concatenate([token_out, numer_back], axis=1)

    for acc in (mid_acc, feature_acc, slice_acc, proj_acc, bias_acc, temp_acc):
        acc[...] = jnp.zeros_like(acc)

    def part(ref, p, size):
        return ref.at[pl.ds(pl.multiple_of(p * size, 8), size), :]

    def start_scatter(src, recv, size, sems):
        return [
            send(part(src, group_peer(k), size), recv.at[k - 1], sems.at[0, k - 1], sems.at[1, k - 1], group_id(k))
            for k in range(1, parts)
        ]

    def start_across(copies, src, recv, z, size, sems):
        total = part(src, group, size)[...]
        for k, copy in enumerate(copies):
            copy.wait()
            total = total + recv[k]
        z[high] = total
        return [
            send(z.at[high], z.at[high], sems.at[2, k - 1], sems.at[3, k - 1], high_id(k))
            for k in range(1, high_n)
        ]

    def start_gather(copies, z, full, size, sems):
        for copy in copies:
            copy.wait()
        total = z[0]
        for k in range(1, high_n):
            total = total + z[k]
        mine = part(full, group, size)
        mine[...] = total
        return [
            send(mine, mine, sems.at[4, k - 1], sems.at[5, k - 1], group_id(k))
            for k in range(1, parts)
        ]

    def second(i, carry):
        at = pl.ds(pl.multiple_of(i * CHUNK, CHUNK), CHUNK)
        both = dot(pb_ref[at, :], mix)
        mixed = both[:, :W].astype(BF16)
        feat_back = both[:, W:]
        rounded = feat_back.astype(BF16)
        mf_ref[at, W:] = rounded
        bias_acc[...] += jnp.sum(feat_back.reshape(CHUNK // 8, 8, W), axis=0)
        proj_acc[...] += dot(gt_ref[i], mixed)
        feature_acc[...] += dot(xt_ref[i], rounded)
        return carry

    def third(i, carry):
        at = pl.ds(pl.multiple_of(i * CHUNK, CHUNK), CHUNK)
        probs = probs_ref[at, :]
        prob_back = dot(fb_ref[at, :], mix, NT) + den_back
        inner = group_sum(probs * prob_back, ones)
        logit_back = probs * (prob_back - inner)
        temp_acc[...] += jnp.sum((logit_back * logits_ref[at, :]).reshape(CHUNK // 8, 8, S), axis=0)
        score_back = (logit_back * inv_s).astype(BF16)
        mid_back = dot(score_back, a_block, NT).astype(BF16)
        mf_ref[at, :W] = mid_back
        mid_acc[...] += dot(xt_ref[i], mid_back)
        slice_acc[...] += dot(midt_ref[i], score_back)
        return carry

    steps = rows // CHUNK
    lax.fori_loop(0, steps, second, 0)
    early_src[0:W, :] = feature_acc[...]
    early_src[W : 2 * W, :] = proj_acc[...].T
    early = start_scatter(early_src, early_recv, early_rows, early_sems)
    lax.fori_loop(0, steps // 2, third, 0)
    early = start_across(early, early_src, early_recv, early_z, early_rows, early_sems)
    lax.fori_loop(steps // 2, steps, third, 0)
    early = start_gather(early, early_z, early_full, early_rows, early_sems)

    late_src[0:W, :] = mid_acc[...]
    slices = fold_rows(jnp.where(same_head, slice_acc[...], 0.0), D)
    slices = slices[:, :W] + slices[:, W:]
    slices = slices + pltpu.roll(slices, 64, 1)
    slices = slices + pltpu.roll(slices, 32, 1)
    lane = iota((D, W), 1)
    owner = (node == 0).astype(F32)
    block = jnp.where(lane < M, slices, 0.0)
    for i in range(3):
        term = fold_rows(d_maps[:, i * W : (i + 1) * W], D)
        for shift in (64, 32, 16):
            term = term + pltpu.roll(term, shift, 1)
        start = M + i * D
        block = jnp.where((lane >= start) & (lane < start + D), term * owner, block)
    late_src[W : W + D, :] = block
    pick_heads = jnp.where(block_of(iota((S, W), 0), M) == iota((S, W), 1), 1.0, 0.0).astype(BF16)
    temp = jnp.sum(dot32(temp_acc[...] * -inv_s, pick_heads), axis=0, keepdims=True)
    bias = jnp.sum(bias_acc[...], axis=0, keepdims=True)
    row = iota((8, W), 0)
    late_src[W + D : W + D + 8, :] = jnp.where(row == 0, bias, jnp.where(row == 1, temp, 0.0))
    used = W + D + 8
    if used < parts * late_rows:
        late_src[used:, :] = jnp.zeros((parts * late_rows - used, W), F32)

    late = start_scatter(late_src, late_recv, late_rows, late_sems)

    def store(i):
        at = pl.ds(pl.multiple_of(i * CHUNK, CHUNK), CHUNK)
        return pltpu.make_async_copy(vertex_ref.at[at, :], vertex_hbm.at[at, :], out_sem.at[i])

    def fourth(i, carry):
        at = pl.ds(pl.multiple_of(i * CHUNK, CHUNK), CHUNK)
        vertex_ref[at, :] = dot(mf_ref[at, :], w12, NT)
        store(i).start()
        return carry

    lax.fori_loop(0, steps // 2, fourth, 0)
    late = start_across(late, late_src, late_recv, late_z, late_rows, late_sems)
    lax.fori_loop(steps // 2, steps, fourth, 0)
    late = start_gather(late, late_z, late_full, late_rows, late_sems)
    for copy in early:
        copy.wait()
    packed_ref[0 : 2 * W, :] = early_full[...]
    for copy in late:
        copy.wait()
    packed_ref[2 * W :, :] = late_full[...]
    for i in range(steps):
        store(i).wait()


def final_kernel(
    packed_ref, vertex_ref,
    out_ref, mid_ref, feature_ref, bias_ref, slice_ref, temp_ref, query_ref, key_ref, value_ref, proj_ref,
    sems,
):
    size = vertex_ref.shape[0] // PIECES
    copies = [
        pltpu.make_async_copy(
            vertex_ref.at[pl.ds(i * size, size), :], out_ref.at[pl.ds(i * size, size), :], sems.at[i]
        )
        for i in range(PIECES)
    ]
    for copy in copies:
        copy.start()
    feature_ref[...] = packed_ref[0:W, :]
    proj_ref[...] = packed_ref[W : 2 * W, :]
    mid_ref[...] = packed_ref[2 * W : 3 * W, :]
    block = packed_ref[3 * W : 3 * W + D, :]
    slice_ref[...] = block[:, 0:M]
    query_ref[...] = block[:, M : M + D]
    key_ref[...] = block[:, M + D : M + 2 * D]
    value_ref[...] = block[:, M + 2 * D : M + 3 * D]
    bias_ref[...] = packed_ref[3 * W + D : 3 * W + D + 1, :]
    temp_ref[...] = packed_ref[3 * W + D + 1 : 3 * W + D + 2, 0:HEADS]
    for copy in copies:
        copy.wait()


def shards(n_member, n_node, x, g, w1, w2, offset, a, s, wq, wk, wv, w3):
    x, g = x[0], g[0]
    rows = x.shape[0]
    high_n = n_node // LOW
    parts = n_member * LOW
    early_rows = -(-2 * W // (8 * parts)) * 8
    late_rows = -(-(W + D + 8) // (8 * parts)) * 8
    packed_rows = 2 * W + parts * late_rows
    assert parts * early_rows == 2 * W and n_node % LOW == 0
    vmem = pl.BlockSpec(memory_space=pltpu.VMEM)
    hbm = pl.BlockSpec(memory_space=pl.ANY)
    dma = pltpu.SemaphoreType.DMA
    flops = 2 * rows * S * S * 12
    packed, vertex = pl.pallas_call(
        functools.partial(main_kernel, n_member, n_node, parts, early_rows, late_rows),
        out_shape=(
            jax.ShapeDtypeStruct((packed_rows, W), F32),
            jax.ShapeDtypeStruct((rows, W), F32),
        ),
        in_specs=[pl.BlockSpec(memory_space=pltpu.SMEM), hbm, hbm] + [vmem] * 8,
        out_specs=(vmem, hbm),
        scratch_shapes=[
            pltpu.VMEM((rows, W), BF16),
            pltpu.VMEM((rows, W), BF16),
            pltpu.VMEM((rows, W), BF16),
            pltpu.VMEM((rows, 2 * W), BF16),
            pltpu.VMEM((rows, S), BF16),
            pltpu.VMEM((rows, S), F32),
            pltpu.VMEM((rows, S), F32),
            pltpu.VMEM((rows, 2 * W), BF16),
            pltpu.VMEM((rows, W), F32),
            pltpu.VMEM((rows // CHUNK, W, CHUNK), BF16),
            pltpu.VMEM((rows // CHUNK, W, CHUNK), BF16),
            pltpu.VMEM((rows // CHUNK, W, CHUNK), BF16),
            pltpu.VMEM((S, 2 * W), F32),
            pltpu.VMEM((8, S), F32),
            pltpu.VMEM((W, W), F32),
            pltpu.VMEM((W, W), F32),
            pltpu.VMEM((W, S), F32),
            pltpu.VMEM((W, W), F32),
            pltpu.VMEM((8, W), F32),
            pltpu.VMEM((8, S), F32),
            pltpu.VMEM((LOW, 24, W), F32),
            pltpu.VMEM((LOW - 1, 24, W), F32),
            pltpu.VMEM((high_n, 24, W), F32),
            pltpu.VMEM((LOW, 24, W), F32),
            pltpu.VMEM((parts * early_rows, W), F32),
            pltpu.VMEM((parts - 1, early_rows, W), F32),
            pltpu.VMEM((high_n, early_rows, W), F32),
            pltpu.VMEM((parts * early_rows, W), F32),
            pltpu.VMEM((parts * late_rows, W), F32),
            pltpu.VMEM((parts - 1, late_rows, W), F32),
            pltpu.VMEM((high_n, late_rows, W), F32),
            pltpu.VMEM((parts * late_rows, W), F32),
            dma((2, rows // CHUNK)),
            dma((rows // CHUNK,)),
            dma((LOW - 1,)), dma((LOW - 1,)),
            dma((high_n - 1,)), dma((high_n - 1,)),
            dma((LOW - 1,)), dma((LOW - 1,)),
            dma((6, max(parts, high_n) - 1)),
            dma((6, max(parts, high_n) - 1)),
        ],
        compiler_params=pltpu.CompilerParams(
            collective_id=0, has_side_effects=True, vmem_limit_bytes=VMEM_LIMIT
        ),
        cost_estimate=pl.CostEstimate(
            flops=flops, bytes_accessed=rows * W * 8, transcendentals=rows * S
        ),
        name="pool_and_gradients",
    )(s, x, g, w1, w2, offset.reshape(1, W), a, wq, wk, wv, w3)

    outs = pl.pallas_call(
        final_kernel,
        out_shape=(
            jax.ShapeDtypeStruct((rows, W), F32),
            jax.ShapeDtypeStruct((W, W), F32),
            jax.ShapeDtypeStruct((W, W), F32),
            jax.ShapeDtypeStruct((1, W), F32),
            jax.ShapeDtypeStruct((D, M), F32),
            jax.ShapeDtypeStruct((1, HEADS), F32),
            jax.ShapeDtypeStruct((D, D), F32),
            jax.ShapeDtypeStruct((D, D), F32),
            jax.ShapeDtypeStruct((D, D), F32),
            jax.ShapeDtypeStruct((W, W), F32),
        ),
        in_specs=[vmem, hbm],
        out_specs=(hbm,) + (vmem,) * 9,
        scratch_shapes=[dma((PIECES,))],
        compiler_params=pltpu.CompilerParams(vmem_limit_bytes=VMEM_LIMIT),
        cost_estimate=pl.CostEstimate(flops=0, bytes_accessed=rows * W * 8, transcendentals=0),
        name="unpack",
    )(packed, vertex)
    vertex, mid, feature, bias, slices, temp, query, key, value, proj = outs
    return (
        vertex[None], mid, feature, bias.reshape(W), slices, temp.reshape(HEADS),
        query, key, value, proj,
    )


def solution(mesh):
    spread = P("member", "node", None)
    return jax.shard_map(
        functools.partial(shards, mesh.shape["member"], mesh.shape["node"]),
        mesh=mesh,
        in_specs=(spread, spread) + (P(),) * 9,
        out_specs=(spread,) + (P(),) * 9,
        check_vma=False,
    )
```

```python
import functools
import math

import jax
import jax.numpy as jnp
from jax import lax
from jax.experimental import pallas as pl
from jax.experimental.pallas import tpu as pltpu
from jax.sharding import PartitionSpec as P

W = 128
HEADS = 8
M = 32
D = 16
S = HEADS * M
LOW = 4
CHUNK = 2048
EPS = 1e-05
PIECES = 8
VMEM_LIMIT = 62 * 1024 * 1024
F32 = jnp.float32
BF16 = jnp.bfloat16
MESH = pl.DeviceIdType.MESH

NN = (((1,), (0,)), ((), ()))
NT = (((1,), (1,)), ((), ()))
TN = (((0,), (0,)), ((), ()))


def dot(a, b, dims=NN):
    return lax.dot_general(a, b, dims, preferred_element_type=F32)


def split(a):
    upper = a.astype(BF16)
    return upper, (a - upper.astype(F32)).astype(BF16)


def dot32(a, b, dims=NN):
    a_parts = (a,) if a.dtype == BF16 else split(a)
    b_parts = (b,) if b.dtype == BF16 else split(b)
    total = dot(a_parts[0], b_parts[0], dims)
    if len(b_parts) == 2:
        total = total + dot(a_parts[0], b_parts[1], dims)
    if len(a_parts) == 2:
        total = total + dot(a_parts[1], b_parts[0], dims)
    return total


def iota(shape, axis):
    return lax.broadcasted_iota(jnp.int32, shape, axis)


def block_of(index, size):
    return index >> (size.bit_length() - 1)


def group_sum(values, ones):
    return dot(jnp.concatenate(split(values), axis=1), ones)


def fold_rows(a, step):
    total = a[0:step]
    for i in range(step, a.shape[0], step):
        total = total + a[i : i + step]
    return total


def main_kernel(
    n_member, n_node, parts, early_rows, late_rows,
    s_ref, x_hbm, g_hbm, w1_ref, w2_ref, off_ref, a_ref, wq_ref, wk_ref, wv_ref, w3_ref,
    packed_ref, vertex_hbm,
    x_ref, g_ref, mid_ref, fb_ref, pb_ref, probs_ref, logits_ref, mf_ref, vertex_ref,
    xt_ref, gt_ref, midt_ref,
    pool_acc, den_acc, mid_acc, feature_acc, slice_acc, proj_acc, bias_acc, temp_acc,
    pool_src, pool_recv, pool_z, pool_full,
    early_src, early_recv, early_z, early_full, late_src, late_recv, late_z, late_full,
    in_sem, out_sem,
    a_send, a_recv, b_send, b_recv, c_send, c_recv,
    early_sems, late_sems,
):
    rows = x_ref.shape[0]
    high_n = n_node // LOW
    member, node = lax.axis_index("member"), lax.axis_index("node")
    low, high = lax.rem(node, LOW), lax.div(node, LOW)
    group = member * LOW + low

    def low_peer(k):
        return lax.rem(low + k, LOW)

    def high_peer(k):
        return lax.rem(high + k, high_n)

    def group_peer(k):
        return lax.rem(group + k, parts)

    def low_id(k):
        return (member, high * LOW + low_peer(k))

    def high_id(k):
        return (member, high_peer(k) * LOW + low)

    def group_id(k):
        peer = group_peer(k)
        return (lax.div(peer, LOW), high * LOW + lax.rem(peer, LOW))

    def load(i):
        at = pl.ds(pl.multiple_of(i * CHUNK, CHUNK), CHUNK)
        return (
            pltpu.make_async_copy(x_hbm.at[at, :], x_ref.at[at, :], in_sem.at[0, i]),
            pltpu.make_async_copy(g_hbm.at[at, :], g_ref.at[at, :], in_sem.at[1, i]),
        )

    for i in range(rows // CHUNK):
        for copy in load(i):
            copy.start()

    barrier = pltpu.get_barrier_semaphore()
    for k in range(1, parts):
        pl.semaphore_signal(barrier, inc=1, device_id=group_id(k), device_id_type=MESH)
    for k in range(1, high_n):
        pl.semaphore_signal(barrier, inc=1, device_id=high_id(k), device_id_type=MESH)

    def send(src, dst, send_sem, recv_sem, target):
        copy = pltpu.make_async_remote_copy(
            src_ref=src, dst_ref=dst, send_sem=send_sem, recv_sem=recv_sem,
            device_id=target, device_id_type=MESH,
        )
        copy.start()
        return copy

    head_of_slice = block_of(iota((1, S), 1), M)
    inv_s = jnp.zeros((1, S), F32)
    for h in range(HEADS):
        inv_s = jnp.where(head_of_slice == h, 1.0 / jnp.full((1, S), s_ref[h], F32), inv_s)
    inside = block_of(iota((S, S), 0), M) == block_of(iota((S, S), 1), M)
    ones = jnp.where(inside, 1.0, 0.0).astype(BF16)
    ones = jnp.concatenate([ones, ones], axis=0)
    same_head = block_of(iota((W, S), 0), D) == block_of(iota((W, S), 1), M)
    pick_rows = jnp.where((iota((W, D), 0) & (D - 1)) == iota((W, D), 1), 1.0, 0.0).astype(BF16)
    pick_slices = jnp.where((iota((M, S), 1) & (M - 1)) == iota((M, S), 0), 1.0, 0.0).astype(BF16)
    pick_columns = jnp.where((iota((D, W), 1) & (D - 1)) == iota((D, W), 0), 1.0, 0.0).astype(BF16)
    a_all = dot(dot(pick_rows, a_ref[...]).astype(BF16), pick_slices)
    a_block = jnp.where(same_head, a_all, 0.0).astype(BF16)
    head_square = block_of(iota((W, W), 0), D) == block_of(iota((W, W), 1), D)

    def square_block(ref):
        return jnp.where(
            head_square, dot(dot(pick_rows, ref[...]).astype(BF16), pick_columns), 0.0
        ).astype(BF16)

    maps = jnp.concatenate([square_block(r) for r in (wq_ref, wk_ref, wv_ref)], axis=1)
    maps_back = maps.T
    w12 = jnp.concatenate([w1_ref[...], w2_ref[...]], axis=1)
    w12_back = w12.T
    w3_back = w3_ref[...].T
    a_back = a_block.T
    offset = off_ref[...]

    pool_acc[...] = jnp.zeros_like(pool_acc)
    den_acc[...] = jnp.zeros_like(den_acc)

    def first(i, carry):
        for copy in load(i):
            copy.wait()
        at = pl.ds(pl.multiple_of(i * CHUNK, CHUNK), CHUNK)
        x = x_ref[at, :]
        both = dot(x, w12)
        mid = both[:, :W].astype(BF16)
        feat = (both[:, W:] + offset).astype(BF16)
        back = dot(g_ref[at, :], w3_back).astype(BF16)
        logits = dot(mid, a_block) * inv_s
        e = jnp.exp(logits)
        total = group_sum(e, ones)
        guess = pl.reciprocal(total, approx=True)
        probs = e * (guess * (2.0 - total * guess))
        pb = probs.astype(BF16)
        fb = jnp.concatenate([back, feat], axis=1)
        mid_ref[at, :] = mid
        fb_ref[at, :] = fb
        pb_ref[at, :] = pb
        probs_ref[at, :] = probs
        logits_ref[at, :] = logits
        pool_acc[...] += dot(pb, fb, TN)
        den_acc[...] += jnp.sum(probs.reshape(CHUNK // 8, 8, S), axis=0)
        return carry

    lax.fori_loop(0, rows // CHUNK, first, 0)

    slice_head = block_of(iota((S, W), 0), M) == block_of(iota((S, W), 1), D)
    token_grad = fold_rows(jnp.where(slice_head, pool_acc[:, :W], 0.0), M)
    numer = fold_rows(jnp.where(slice_head, pool_acc[:, W:], 0.0), M)
    den = jnp.sum(den_acc[...], axis=0, keepdims=True)
    for p in range(LOW):
        pool_src[p, 0:8, :] = numer[8 * p : 8 * p + 8]
        pool_src[p, 8:16, :] = token_grad[8 * p : 8 * p + 8]
        piece = den[:, (p % 2) * W : (p % 2 + 1) * W]
        pool_src[p, 16:24, :] = jnp.broadcast_to(piece, (8, W))

    pl.semaphore_wait(barrier, parts - 1 + high_n - 1)

    copies = [
        send(pool_src.at[low_peer(k)], pool_recv.at[k - 1], a_send.at[k - 1], a_recv.at[k - 1], low_id(k))
        for k in range(1, LOW)
    ]
    def turn(source, target):
        def step(i, carry):
            at = pl.ds(pl.multiple_of(i * CHUNK, CHUNK), CHUNK)
            target[i] = source[at, :].T
            return carry

        lax.fori_loop(0, rows // CHUNK, step, 0)

    turn(x_ref, xt_ref)
    total = pool_src[low]
    for k, copy in enumerate(copies):
        copy.wait()
        total = total + pool_recv[k]
    pool_z[high] = total
    copies = [
        send(pool_z.at[high], pool_z.at[high], b_send.at[k - 1], b_recv.at[k - 1], high_id(k))
        for k in range(1, high_n)
    ]
    turn(g_ref, gt_ref)
    turn(mid_ref, midt_ref)
    for copy in copies:
        copy.wait()
    total = pool_z[0]
    for k in range(1, high_n):
        total = total + pool_z[k]
    pool_full[low] = total
    copies = [
        send(pool_full.at[low], pool_full.at[low], c_send.at[k - 1], c_recv.at[k - 1], low_id(k))
        for k in range(1, LOW)
    ]
    for copy in copies:
        copy.wait()

    numer = jnp.concatenate([pool_full[p, 0:8, :] for p in range(LOW)], axis=0)
    token_grad = jnp.concatenate([pool_full[p, 8:16, :] for p in range(LOW)], axis=0)
    den = jnp.concatenate([pool_full[p, 16:17, :] for p in range(2)], axis=1)
    eye = iota((S, S), 0) == iota((S, S), 1)
    den = jnp.sum(jnp.where(eye, den, 0.0), axis=1, keepdims=True)
    inverse = 1.0 / (den + EPS)
    numer = jnp.where(slice_head, jnp.concatenate([numer] * HEADS, axis=0), 0.0)
    token_grad = jnp.where(slice_head, jnp.concatenate([token_grad] * HEADS, axis=0), 0.0)
    tokens = numer / (den + EPS)
    qkv = dot32(tokens, maps)
    q, k, v = qkv[:, :W], qkv[:, W : 2 * W], qkv[:, 2 * W :]
    scale = 1.0 / math.sqrt(D)
    scores = jnp.where(inside, dot32(q, k, NT) * scale, 0.0)
    e = jnp.where(inside, jnp.exp(scores), 0.0)
    share = e / jnp.sum(e, axis=1, keepdims=True)
    token_out = dot32(share, v).astype(BF16)
    d_share = dot32(token_grad, v, NT)
    d_scores = share * (d_share - jnp.sum(share * d_share, axis=1, keepdims=True)) * scale
    d_qkv = jnp.concatenate(
        [dot32(d_scores, k), dot32(d_scores, q, TN), dot32(share, token_grad, TN)], axis=1
    )
    tok_back = dot32(d_qkv, maps_back)
    numer_back = (tok_back * inverse).astype(BF16)
    den_back = -jnp.sum(tok_back * tokens, axis=1, keepdims=True) * inverse
    den_back = jnp.sum(jnp.where(eye, den_back, 0.0), axis=0, keepdims=True)
    d_maps = dot32(tokens, d_qkv, TN)
    mix = jnp.concatenate([token_out, numer_back], axis=1)
    mix_back = mix.T

    for acc in (mid_acc, feature_acc, slice_acc, proj_acc, bias_acc, temp_acc):
        acc[...] = jnp.zeros_like(acc)

    def part(ref, p, size):
        return ref.at[pl.ds(pl.multiple_of(p * size, 8), size), :]

    def start_scatter(src, recv, size, sems):
        return [
            send(part(src, group_peer(k), size), recv.at[k - 1], sems.at[0, k - 1], sems.at[1, k - 1], group_id(k))
            for k in range(1, parts)
        ]

    def start_across(copies, src, recv, z, size, sems):
        total = part(src, group, size)[...]
        for k, copy in enumerate(copies):
            copy.wait()
            total = total + recv[k]
        z[high] = total
        return [
            send(z.at[high], z.at[high], sems.at[2, k - 1], sems.at[3, k - 1], high_id(k))
            for k in range(1, high_n)
        ]

    def start_gather(copies, z, full, size, sems):
        for copy in copies:
            copy.wait()
        total = z[0]
        for k in range(1, high_n):
            total = total + z[k]
        mine = part(full, group, size)
        mine[...] = total
        return [
            send(mine, mine, sems.at[4, k - 1], sems.at[5, k - 1], group_id(k))
            for k in range(1, parts)
        ]

    def second(i, carry):
        at = pl.ds(pl.multiple_of(i * CHUNK, CHUNK), CHUNK)
        both = dot(pb_ref[at, :], mix)
        mixed = both[:, :W].astype(BF16)
        feat_back = both[:, W:]
        rounded = feat_back.astype(BF16)
        mf_ref[at, W:] = rounded
        bias_acc[...] += jnp.sum(feat_back.reshape(CHUNK // 8, 8, W), axis=0)
        proj_acc[...] += dot(gt_ref[i], mixed)
        feature_acc[...] += dot(xt_ref[i], rounded)
        return carry

    def third(i, carry):
        at = pl.ds(pl.multiple_of(i * CHUNK, CHUNK), CHUNK)
        probs = probs_ref[at, :]
        prob_back = dot(fb_ref[at, :], mix_back) + den_back
        inner = group_sum(probs * prob_back, ones)
        logit_back = probs * (prob_back - inner)
        temp_acc[...] += jnp.sum((logit_back * logits_ref[at, :]).reshape(CHUNK // 8, 8, S), axis=0)
        score_back = (logit_back * inv_s).astype(BF16)
        mid_back = dot(score_back, a_back).astype(BF16)
        mf_ref[at, :W] = mid_back
        mid_acc[...] += dot(xt_ref[i], mid_back)
        slice_acc[...] += dot(midt_ref[i], score_back)
        return carry

    steps = rows // CHUNK
    lax.fori_loop(0, steps, second, 0)
    early_src[0:W, :] = feature_acc[...]
    early_src[W : 2 * W, :] = proj_acc[...].T
    early = start_scatter(early_src, early_recv, early_rows, early_sems)
    lax.fori_loop(0, steps // 2, third, 0)
    early = start_across(early, early_src, early_recv, early_z, early_rows, early_sems)
    lax.fori_loop(steps // 2, steps, third, 0)
    early = start_gather(early, early_z, early_full, early_rows, early_sems)

    late_src[0:W, :] = mid_acc[...]
    slices = fold_rows(jnp.where(same_head, slice_acc[...], 0.0), D)
    slices = slices[:, :W] + slices[:, W:]
    slices = slices + pltpu.roll(slices, 64, 1)
    slices = slices + pltpu.roll(slices, 32, 1)
    lane = iota((D, W), 1)
    owner = (node == 0).astype(F32)
    block = jnp.where(lane < M, slices, 0.0)
    for i in range(3):
        term = fold_rows(d_maps[:, i * W : (i + 1) * W], D)
        for shift in (64, 32, 16):
            term = term + pltpu.roll(term, shift, 1)
        start = M + i * D
        block = jnp.where((lane >= start) & (lane < start + D), term * owner, block)
    late_src[W : W + D, :] = block
    pick_heads = jnp.where(block_of(iota((S, W), 0), M) == iota((S, W), 1), 1.0, 0.0).astype(BF16)
    temp = jnp.sum(dot32(temp_acc[...] * -inv_s, pick_heads), axis=0, keepdims=True)
    bias = jnp.sum(bias_acc[...], axis=0, keepdims=True)
    row = iota((8, W), 0)
    late_src[W + D : W + D + 8, :] = jnp.where(row == 0, bias, jnp.where(row == 1, temp, 0.0))
    used = W + D + 8
    if used < parts * late_rows:
        late_src[used:, :] = jnp.zeros((parts * late_rows - used, W), F32)

    late = start_scatter(late_src, late_recv, late_rows, late_sems)

    def store(i):
        at = pl.ds(pl.multiple_of(i * CHUNK, CHUNK), CHUNK)
        return pltpu.make_async_copy(vertex_ref.at[at, :], vertex_hbm.at[at, :], out_sem.at[i])

    def fourth(i, carry):
        at = pl.ds(pl.multiple_of(i * CHUNK, CHUNK), CHUNK)
        vertex_ref[at, :] = dot(mf_ref[at, :], w12_back)
        store(i).start()
        return carry

    lax.fori_loop(0, steps // 2, fourth, 0)
    late = start_across(late, late_src, late_recv, late_z, late_rows, late_sems)
    lax.fori_loop(steps // 2, steps, fourth, 0)
    late = start_gather(late, late_z, late_full, late_rows, late_sems)
    for copy in early:
        copy.wait()
    packed_ref[0 : 2 * W, :] = early_full[...]
    for copy in late:
        copy.wait()
    packed_ref[2 * W :, :] = late_full[...]
    for i in range(steps):
        store(i).wait()


def final_kernel(
    packed_ref, vertex_ref,
    out_ref, mid_ref, feature_ref, bias_ref, slice_ref, temp_ref, query_ref, key_ref, value_ref, proj_ref,
    held, sems,
):
    size = vertex_ref.shape[0] // PIECES
    pieces = [pl.ds(i * size, size) for i in range(PIECES)]
    loads = [
        pltpu.make_async_copy(vertex_ref.at[at, :], held.at[at, :], sems.at[0, i])
        for i, at in enumerate(pieces)
    ]
    copies = [
        pltpu.make_async_copy(held.at[at, :], out_ref.at[at, :], sems.at[1, i])
        for i, at in enumerate(pieces)
    ]
    for copy in loads:
        copy.start()
    for before, copy in zip(loads, copies):
        before.wait()
        copy.start()
    feature_ref[...] = packed_ref[0:W, :]
    proj_ref[...] = packed_ref[W : 2 * W, :]
    mid_ref[...] = packed_ref[2 * W : 3 * W, :]
    block = packed_ref[3 * W : 3 * W + D, :]
    slice_ref[...] = block[:, 0:M]
    query_ref[...] = block[:, M : M + D]
    key_ref[...] = block[:, M + D : M + 2 * D]
    value_ref[...] = block[:, M + 2 * D : M + 3 * D]
    bias_ref[...] = packed_ref[3 * W + D : 3 * W + D + 1, :]
    temp_ref[...] = packed_ref[3 * W + D + 1 : 3 * W + D + 2, 0:HEADS]
    for copy in copies:
        copy.wait()


def shards(n_member, n_node, x, g, w1, w2, offset, a, s, wq, wk, wv, w3):
    x, g = x[0], g[0]
    rows = x.shape[0]
    high_n = n_node // LOW
    parts = n_member * LOW
    early_rows = -(-2 * W // (8 * parts)) * 8
    late_rows = -(-(W + D + 8) // (8 * parts)) * 8
    packed_rows = 2 * W + parts * late_rows
    assert parts * early_rows == 2 * W and n_node % LOW == 0
    vmem = pl.BlockSpec(memory_space=pltpu.VMEM)
    hbm = pl.BlockSpec(memory_space=pl.ANY)
    dma = pltpu.SemaphoreType.DMA
    flops = 2 * rows * S * S * 12
    packed, vertex = pl.pallas_call(
        functools.partial(main_kernel, n_member, n_node, parts, early_rows, late_rows),
        out_shape=(
            jax.ShapeDtypeStruct((packed_rows, W), F32),
            jax.ShapeDtypeStruct((rows, W), F32),
        ),
        in_specs=[pl.BlockSpec(memory_space=pltpu.SMEM), hbm, hbm] + [vmem] * 8,
        out_specs=(vmem, hbm),
        scratch_shapes=[
            pltpu.VMEM((rows, W), BF16),
            pltpu.VMEM((rows, W), BF16),
            pltpu.VMEM((rows, W), BF16),
            pltpu.VMEM((rows, 2 * W), BF16),
            pltpu.VMEM((rows, S), BF16),
            pltpu.VMEM((rows, S), F32),
            pltpu.VMEM((rows, S), F32),
            pltpu.VMEM((rows, 2 * W), BF16),
            pltpu.VMEM((rows, W), F32),
            pltpu.VMEM((rows // CHUNK, W, CHUNK), BF16),
            pltpu.VMEM((rows // CHUNK, W, CHUNK), BF16),
            pltpu.VMEM((rows // CHUNK, W, CHUNK), BF16),
            pltpu.VMEM((S, 2 * W), F32),
            pltpu.VMEM((8, S), F32),
            pltpu.VMEM((W, W), F32),
            pltpu.VMEM((W, W), F32),
            pltpu.VMEM((W, S), F32),
            pltpu.VMEM((W, W), F32),
            pltpu.VMEM((8, W), F32),
            pltpu.VMEM((8, S), F32),
            pltpu.VMEM((LOW, 24, W), F32),
            pltpu.VMEM((LOW - 1, 24, W), F32),
            pltpu.VMEM((high_n, 24, W), F32),
            pltpu.VMEM((LOW, 24, W), F32),
            pltpu.VMEM((parts * early_rows, W), F32),
            pltpu.VMEM((parts - 1, early_rows, W), F32),
            pltpu.VMEM((high_n, early_rows, W), F32),
            pltpu.VMEM((parts * early_rows, W), F32),
            pltpu.VMEM((parts * late_rows, W), F32),
            pltpu.VMEM((parts - 1, late_rows, W), F32),
            pltpu.VMEM((high_n, late_rows, W), F32),
            pltpu.VMEM((parts * late_rows, W), F32),
            dma((2, rows // CHUNK)),
            dma((rows // CHUNK,)),
            dma((LOW - 1,)), dma((LOW - 1,)),
            dma((high_n - 1,)), dma((high_n - 1,)),
            dma((LOW - 1,)), dma((LOW - 1,)),
            dma((6, max(parts, high_n) - 1)),
            dma((6, max(parts, high_n) - 1)),
        ],
        compiler_params=pltpu.CompilerParams(
            collective_id=0, has_side_effects=True, vmem_limit_bytes=VMEM_LIMIT
        ),
        cost_estimate=pl.CostEstimate(
            flops=flops, bytes_accessed=rows * W * 8, transcendentals=rows * S
        ),
        name="pool_and_gradients",
    )(s, x, g, w1, w2, offset.reshape(1, W), a, wq, wk, wv, w3)

    outs = pl.pallas_call(
        final_kernel,
        out_shape=(
            jax.ShapeDtypeStruct((rows, W), F32),
            jax.ShapeDtypeStruct((W, W), F32),
            jax.ShapeDtypeStruct((W, W), F32),
            jax.ShapeDtypeStruct((1, W), F32),
            jax.ShapeDtypeStruct((D, M), F32),
            jax.ShapeDtypeStruct((1, HEADS), F32),
            jax.ShapeDtypeStruct((D, D), F32),
            jax.ShapeDtypeStruct((D, D), F32),
            jax.ShapeDtypeStruct((D, D), F32),
            jax.ShapeDtypeStruct((W, W), F32),
        ),
        in_specs=[vmem, hbm],
        out_specs=(hbm,) + (vmem,) * 9,
        scratch_shapes=[pltpu.VMEM((rows, W), F32), dma((2, PIECES))],
        compiler_params=pltpu.CompilerParams(vmem_limit_bytes=VMEM_LIMIT),
        cost_estimate=pl.CostEstimate(flops=0, bytes_accessed=rows * W * 8, transcendentals=0),
        name="unpack",
    )(packed, vertex)
    vertex, mid, feature, bias, slices, temp, query, key, value, proj = outs
    return (
        vertex[None], mid, feature, bias.reshape(W), slices, temp.reshape(HEADS),
        query, key, value, proj,
    )


def solution(mesh):
    spread = P("member", "node", None)
    return jax.shard_map(
        functools.partial(shards, mesh.shape["member"], mesh.shape["node"]),
        mesh=mesh,
        in_specs=(spread, spread) + (P(),) * 9,
        out_specs=(spread,) + (P(),) * 9,
        check_vma=False,
    )
```

```python
import functools
import math

import jax
import jax.numpy as jnp
from jax import lax
from jax.experimental import pallas as pl
from jax.experimental.pallas import tpu as pltpu
from jax.sharding import PartitionSpec as P

W = 128
HEADS = 8
M = 32
D = 16
S = HEADS * M
LOW = 4
CHUNK = 2048
EPS = 1e-05
PIECES = 8
VMEM_LIMIT = 62 * 1024 * 1024
F32 = jnp.float32
BF16 = jnp.bfloat16
MESH = pl.DeviceIdType.MESH

NN = (((1,), (0,)), ((), ()))
NT = (((1,), (1,)), ((), ()))
TN = (((0,), (0,)), ((), ()))


def dot(a, b, dims=NN):
    return lax.dot_general(a, b, dims, preferred_element_type=F32)


def split(a):
    upper = a.astype(BF16)
    return upper, (a - upper.astype(F32)).astype(BF16)


def dot32(a, b, dims=NN):
    a_parts = (a,) if a.dtype == BF16 else split(a)
    b_parts = (b,) if b.dtype == BF16 else split(b)
    total = dot(a_parts[0], b_parts[0], dims)
    if len(b_parts) == 2:
        total = total + dot(a_parts[0], b_parts[1], dims)
    if len(a_parts) == 2:
        total = total + dot(a_parts[1], b_parts[0], dims)
    return total


def iota(shape, axis):
    return lax.broadcasted_iota(jnp.int32, shape, axis)


def block_of(index, size):
    return index >> (size.bit_length() - 1)


def group_sum(values, ones):
    return dot(jnp.concatenate(split(values), axis=1), ones)


def fold_rows(a, step):
    total = a[0:step]
    for i in range(step, a.shape[0], step):
        total = total + a[i : i + step]
    return total


def main_kernel(
    n_member, n_node, parts, early_rows, late_rows,
    s_ref, x_hbm, g_hbm, w1_ref, w2_ref, off_ref, a_ref, wq_ref, wk_ref, wv_ref, w3_ref,
    packed_ref, vertex_hbm,
    x_ref, g_ref, mid_ref, fb_ref, pb_ref, probs_ref, logits_ref, mf_ref, vertex_ref,
    gxt_ref, midt_ref,
    pool_acc, den_acc, mid_acc, second_acc, slice_acc, bias_acc, temp_acc,
    pool_src, pool_recv, pool_z, pool_full,
    early_src, early_recv, early_z, early_full, late_src, late_recv, late_z, late_full,
    in_sem, out_sem,
    a_send, a_recv, b_send, b_recv, c_send, c_recv,
    early_sems, late_sems,
):
    rows = x_ref.shape[0]
    high_n = n_node // LOW
    member, node = lax.axis_index("member"), lax.axis_index("node")
    low, high = lax.rem(node, LOW), lax.div(node, LOW)
    group = member * LOW + low

    def low_peer(k):
        return lax.rem(low + k, LOW)

    def high_peer(k):
        return lax.rem(high + k, high_n)

    def group_peer(k):
        return lax.rem(group + k, parts)

    def low_id(k):
        return (member, high * LOW + low_peer(k))

    def high_id(k):
        return (member, high_peer(k) * LOW + low)

    def group_id(k):
        peer = group_peer(k)
        return (lax.div(peer, LOW), high * LOW + lax.rem(peer, LOW))

    def load(i):
        at = pl.ds(pl.multiple_of(i * CHUNK, CHUNK), CHUNK)
        return (
            pltpu.make_async_copy(x_hbm.at[at, :], x_ref.at[at, :], in_sem.at[0, i]),
            pltpu.make_async_copy(g_hbm.at[at, :], g_ref.at[at, :], in_sem.at[1, i]),
        )

    for i in range(rows // CHUNK):
        for copy in load(i):
            copy.start()

    barrier = pltpu.get_barrier_semaphore()
    for k in range(1, parts):
        pl.semaphore_signal(barrier, inc=1, device_id=group_id(k), device_id_type=MESH)
    for k in range(1, high_n):
        pl.semaphore_signal(barrier, inc=1, device_id=high_id(k), device_id_type=MESH)

    def send(src, dst, send_sem, recv_sem, target):
        copy = pltpu.make_async_remote_copy(
            src_ref=src, dst_ref=dst, send_sem=send_sem, recv_sem=recv_sem,
            device_id=target, device_id_type=MESH,
        )
        copy.start()
        return copy

    head_of_slice = block_of(iota((1, S), 1), M)
    inv_s = jnp.zeros((1, S), F32)
    for h in range(HEADS):
        inv_s = jnp.where(head_of_slice == h, 1.0 / jnp.full((1, S), s_ref[h], F32), inv_s)
    inside = block_of(iota((S, S), 0), M) == block_of(iota((S, S), 1), M)
    ones = jnp.where(inside, 1.0, 0.0).astype(BF16)
    ones = jnp.concatenate([ones, ones], axis=0)
    same_head = block_of(iota((W, S), 0), D) == block_of(iota((W, S), 1), M)
    pick_rows = jnp.where((iota((W, D), 0) & (D - 1)) == iota((W, D), 1), 1.0, 0.0).astype(BF16)
    pick_slices = jnp.where((iota((M, S), 1) & (M - 1)) == iota((M, S), 0), 1.0, 0.0).astype(BF16)
    pick_columns = jnp.where((iota((D, W), 1) & (D - 1)) == iota((D, W), 0), 1.0, 0.0).astype(BF16)
    a_all = dot(dot(pick_rows, a_ref[...]).astype(BF16), pick_slices)
    a_block = jnp.where(same_head, a_all, 0.0).astype(BF16)
    head_square = block_of(iota((W, W), 0), D) == block_of(iota((W, W), 1), D)

    def square_block(ref):
        return jnp.where(
            head_square, dot(dot(pick_rows, ref[...]).astype(BF16), pick_columns), 0.0
        ).astype(BF16)

    maps = jnp.concatenate([square_block(r) for r in (wq_ref, wk_ref, wv_ref)], axis=1)
    maps_back = maps.T
    w12 = jnp.concatenate([w1_ref[...], w2_ref[...]], axis=1)
    w12_back = w12.T
    w3_back = w3_ref[...].T
    a_back = a_block.T
    offset = off_ref[...]

    pool_acc[...] = jnp.zeros_like(pool_acc)
    den_acc[...] = jnp.zeros_like(den_acc)

    def first(i, carry):
        for copy in load(i):
            copy.wait()
        at = pl.ds(pl.multiple_of(i * CHUNK, CHUNK), CHUNK)
        x = x_ref[at, :]
        both = dot(x, w12)
        mid = both[:, :W].astype(BF16)
        feat = (both[:, W:] + offset).astype(BF16)
        back = dot(g_ref[at, :], w3_back).astype(BF16)
        logits = dot(mid, a_block) * inv_s
        e = jnp.exp(logits)
        total = group_sum(e, ones)
        guess = pl.reciprocal(total, approx=True)
        probs = e * (guess * (2.0 - total * guess))
        pb = probs.astype(BF16)
        fb = jnp.concatenate([back, feat], axis=1)
        mid_ref[at, :] = mid
        fb_ref[at, :] = fb
        pb_ref[at, :] = pb
        probs_ref[at, :] = probs
        logits_ref[at, :] = logits
        pool_acc[...] += dot(pb, fb, TN)
        den_acc[...] += jnp.sum(probs.reshape(CHUNK // 8, 8, S), axis=0)
        return carry

    lax.fori_loop(0, rows // CHUNK, first, 0)

    slice_head = block_of(iota((S, W), 0), M) == block_of(iota((S, W), 1), D)
    token_grad = fold_rows(jnp.where(slice_head, pool_acc[:, :W], 0.0), M)
    numer = fold_rows(jnp.where(slice_head, pool_acc[:, W:], 0.0), M)
    den = jnp.sum(den_acc[...], axis=0, keepdims=True)
    for p in range(LOW):
        pool_src[p, 0:8, :] = numer[8 * p : 8 * p + 8]
        pool_src[p, 8:16, :] = token_grad[8 * p : 8 * p + 8]
        piece = den[:, (p % 2) * W : (p % 2 + 1) * W]
        pool_src[p, 16:24, :] = jnp.broadcast_to(piece, (8, W))

    pl.semaphore_wait(barrier, parts - 1 + high_n - 1)

    copies = [
        send(pool_src.at[low_peer(k)], pool_recv.at[k - 1], a_send.at[k - 1], a_recv.at[k - 1], low_id(k))
        for k in range(1, LOW)
    ]
    def turn(source, target, start):
        def step(i, carry):
            at = pl.ds(pl.multiple_of(i * CHUNK, CHUNK), CHUNK)
            target[i, start : start + W, :] = source[at, :].T
            return carry

        lax.fori_loop(0, rows // CHUNK, step, 0)

    turn(x_ref, gxt_ref, W)
    total = pool_src[low]
    for k, copy in enumerate(copies):
        copy.wait()
        total = total + pool_recv[k]
    pool_z[high] = total
    copies = [
        send(pool_z.at[high], pool_z.at[high], b_send.at[k - 1], b_recv.at[k - 1], high_id(k))
        for k in range(1, high_n)
    ]
    turn(g_ref, gxt_ref, 0)
    for copy in copies:
        copy.wait()
    total = pool_z[0]
    for k in range(1, high_n):
        total = total + pool_z[k]
    pool_full[low] = total
    copies = [
        send(pool_full.at[low], pool_full.at[low], c_send.at[k - 1], c_recv.at[k - 1], low_id(k))
        for k in range(1, LOW)
    ]
    turn(mid_ref, midt_ref, 0)
    for copy in copies:
        copy.wait()

    numer = jnp.concatenate([pool_full[p, 0:8, :] for p in range(LOW)], axis=0)
    token_grad = jnp.concatenate([pool_full[p, 8:16, :] for p in range(LOW)], axis=0)
    den = jnp.concatenate([pool_full[p, 16:17, :] for p in range(2)], axis=1)
    eye = iota((S, S), 0) == iota((S, S), 1)
    den = jnp.sum(jnp.where(eye, den, 0.0), axis=1, keepdims=True)
    inverse = 1.0 / (den + EPS)
    numer = jnp.where(slice_head, jnp.concatenate([numer] * HEADS, axis=0), 0.0)
    token_grad = jnp.where(slice_head, jnp.concatenate([token_grad] * HEADS, axis=0), 0.0)
    tokens = numer / (den + EPS)
    qkv = dot32(tokens, maps)
    q, k, v = qkv[:, :W], qkv[:, W : 2 * W], qkv[:, 2 * W :]
    scale = 1.0 / math.sqrt(D)
    scores = jnp.where(inside, dot32(q, k, NT) * scale, 0.0)
    e = jnp.where(inside, jnp.exp(scores), 0.0)
    share = e / jnp.sum(e, axis=1, keepdims=True)
    token_out = dot32(share, v).astype(BF16)
    d_share = dot32(token_grad, v, NT)
    d_scores = share * (d_share - jnp.sum(share * d_share, axis=1, keepdims=True)) * scale
    d_qkv = jnp.concatenate(
        [dot32(d_scores, k), dot32(d_scores, q, TN), dot32(share, token_grad, TN)], axis=1
    )
    tok_back = dot32(d_qkv, maps_back)
    numer_back = (tok_back * inverse).astype(BF16)
    den_back = -jnp.sum(tok_back * tokens, axis=1, keepdims=True) * inverse
    den_back = jnp.sum(jnp.where(eye, den_back, 0.0), axis=0, keepdims=True)
    d_maps = dot32(tokens, d_qkv, TN)
    mix = jnp.concatenate([token_out, numer_back], axis=1)
    mix_back = mix.T

    for acc in (mid_acc, second_acc, slice_acc, bias_acc, temp_acc):
        acc[...] = jnp.zeros_like(acc)

    def part(ref, p, size):
        return ref.at[pl.ds(pl.multiple_of(p * size, 8), size), :]

    def start_scatter(src, recv, size, sems):
        return [
            send(part(src, group_peer(k), size), recv.at[k - 1], sems.at[0, k - 1], sems.at[1, k - 1], group_id(k))
            for k in range(1, parts)
        ]

    def start_across(copies, src, recv, z, size, sems):
        total = part(src, group, size)[...]
        for k, copy in enumerate(copies):
            copy.wait()
            total = total + recv[k]
        z[high] = total
        return [
            send(z.at[high], z.at[high], sems.at[2, k - 1], sems.at[3, k - 1], high_id(k))
            for k in range(1, high_n)
        ]

    def start_gather(copies, z, full, size, sems):
        for copy in copies:
            copy.wait()
        total = z[0]
        for k in range(1, high_n):
            total = total + z[k]
        mine = part(full, group, size)
        mine[...] = total
        return [
            send(mine, mine, sems.at[4, k - 1], sems.at[5, k - 1], group_id(k))
            for k in range(1, parts)
        ]

    def second(i, carry):
        at = pl.ds(pl.multiple_of(i * CHUNK, CHUNK), CHUNK)
        both = dot(pb_ref[at, :], mix)
        rounded = both.astype(BF16)
        feat_back = both[:, W:]
        mf_ref[at, W:] = rounded[:, W:]
        bias_acc[...] += jnp.sum(feat_back.reshape(CHUNK // 8, 8, W), axis=0)
        second_acc[...] += dot(gxt_ref[i], rounded)
        return carry

    def third(i, carry):
        at = pl.ds(pl.multiple_of(i * CHUNK, CHUNK), CHUNK)
        probs = probs_ref[at, :]
        prob_back = dot(fb_ref[at, :], mix_back) + den_back
        inner = group_sum(probs * prob_back, ones)
        logit_back = probs * (prob_back - inner)
        temp_acc[...] += jnp.sum((logit_back * logits_ref[at, :]).reshape(CHUNK // 8, 8, S), axis=0)
        score_back = (logit_back * inv_s).astype(BF16)
        mid_back = dot(score_back, a_back).astype(BF16)
        mf_ref[at, :W] = mid_back
        mid_acc[...] += dot(gxt_ref[i, W:, :], mid_back)
        slice_acc[...] += dot(midt_ref[i], score_back)
        return carry

    steps = rows // CHUNK
    lax.fori_loop(0, steps, second, 0)
    early_src[0:W, :] = second_acc[W:, W:]
    early_src[W : 2 * W, :] = second_acc[:W, :W].T
    early = start_scatter(early_src, early_recv, early_rows, early_sems)
    lax.fori_loop(0, steps // 2, third, 0)
    early = start_across(early, early_src, early_recv, early_z, early_rows, early_sems)
    lax.fori_loop(steps // 2, steps, third, 0)
    early = start_gather(early, early_z, early_full, early_rows, early_sems)

    late_src[0:W, :] = mid_acc[...]
    slices = fold_rows(jnp.where(same_head, slice_acc[...], 0.0), D)
    slices = slices[:, :W] + slices[:, W:]
    slices = slices + pltpu.roll(slices, 64, 1)
    slices = slices + pltpu.roll(slices, 32, 1)
    lane = iota((D, W), 1)
    owner = (node == 0).astype(F32)
    block = jnp.where(lane < M, slices, 0.0)
    for i in range(3):
        term = fold_rows(d_maps[:, i * W : (i + 1) * W], D)
        for shift in (64, 32, 16):
            term = term + pltpu.roll(term, shift, 1)
        start = M + i * D
        block = jnp.where((lane >= start) & (lane < start + D), term * owner, block)
    late_src[W : W + D, :] = block
    pick_heads = jnp.where(block_of(iota((S, W), 0), M) == iota((S, W), 1), 1.0, 0.0).astype(BF16)
    temp = jnp.sum(dot32(temp_acc[...] * -inv_s, pick_heads), axis=0, keepdims=True)
    bias = jnp.sum(bias_acc[...], axis=0, keepdims=True)
    row = iota((8, W), 0)
    late_src[W + D : W + D + 8, :] = jnp.where(row == 0, bias, jnp.where(row == 1, temp, 0.0))
    used = W + D + 8
    if used < parts * late_rows:
        late_src[used:, :] = jnp.zeros((parts * late_rows - used, W), F32)

    late = start_scatter(late_src, late_recv, late_rows, late_sems)

    def store(i):
        at = pl.ds(pl.multiple_of(i * CHUNK, CHUNK), CHUNK)
        return pltpu.make_async_copy(vertex_ref.at[at, :], vertex_hbm.at[at, :], out_sem.at[i])

    def fourth(i, carry):
        at = pl.ds(pl.multiple_of(i * CHUNK, CHUNK), CHUNK)
        vertex_ref[at, :] = dot(mf_ref[at, :], w12_back)
        store(i).start()
        return carry

    lax.fori_loop(0, steps // 2, fourth, 0)
    late = start_across(late, late_src, late_recv, late_z, late_rows, late_sems)
    lax.fori_loop(steps // 2, steps, fourth, 0)
    late = start_gather(late, late_z, late_full, late_rows, late_sems)
    for copy in early:
        copy.wait()
    packed_ref[0 : 2 * W, :] = early_full[...]
    for copy in late:
        copy.wait()
    packed_ref[2 * W :, :] = late_full[...]
    for i in range(steps):
        store(i).wait()


def final_kernel(
    packed_ref, vertex_ref,
    out_ref, mid_ref, feature_ref, bias_ref, slice_ref, temp_ref, query_ref, key_ref, value_ref, proj_ref,
    packed, held, slice_out, query_out, key_out, value_out, load_sems, store_sems, small_sems,
):
    size = vertex_ref.shape[0] // PIECES
    pieces = [pl.ds(i * size, size) for i in range(PIECES)]
    loads = [
        pltpu.make_async_copy(vertex_ref.at[at, :], held.at[at, :], load_sems.at[i])
        for i, at in enumerate(pieces)
    ]
    copies = [
        pltpu.make_async_copy(held.at[at, :], out_ref.at[at, :], store_sems.at[i])
        for i, at in enumerate(pieces)
    ]
    load_packed = pltpu.make_async_copy(packed_ref, packed, load_sems.at[PIECES])
    load_packed.start()
    for copy in loads:
        copy.start()
    load_packed.wait()
    block = packed[3 * W : 3 * W + D, :]
    slice_out[...] = block[:, 0:M]
    query_out[...] = block[:, M : M + D]
    key_out[...] = block[:, M + D : M + 2 * D]
    value_out[...] = block[:, M + 2 * D : M + 3 * D]
    last = 3 * W + D
    bias_ref[...] = packed[last : last + 1, :]
    temp_ref[...] = packed[last + 1 : last + 2, 0:HEADS]
    smalls = [
        (packed.at[0:W, :], feature_ref),
        (packed.at[W : 2 * W, :], proj_ref),
        (packed.at[2 * W : 3 * W, :], mid_ref),
        (slice_out, slice_ref),
        (query_out, query_ref),
        (key_out, key_ref),
        (value_out, value_ref),
    ]
    smalls = [
        pltpu.make_async_copy(source, target, small_sems.at[i])
        for i, (source, target) in enumerate(smalls)
    ]
    for copy in smalls:
        copy.start()
    for before, copy in zip(loads, copies):
        before.wait()
        copy.start()
    for copy in smalls + copies:
        copy.wait()


def shards(n_member, n_node, x, g, w1, w2, offset, a, s, wq, wk, wv, w3):
    x, g = x[0], g[0]
    rows = x.shape[0]
    high_n = n_node // LOW
    parts = n_member * LOW
    early_rows = -(-2 * W // (8 * parts)) * 8
    late_rows = -(-(W + D + 8) // (8 * parts)) * 8
    packed_rows = 2 * W + parts * late_rows
    assert parts * early_rows == 2 * W and n_node % LOW == 0
    vmem = pl.BlockSpec(memory_space=pltpu.VMEM)
    hbm = pl.BlockSpec(memory_space=pl.ANY)
    dma = pltpu.SemaphoreType.DMA
    flops = 2 * rows * S * S * 12
    packed, vertex = pl.pallas_call(
        functools.partial(main_kernel, n_member, n_node, parts, early_rows, late_rows),
        out_shape=(
            jax.ShapeDtypeStruct((packed_rows, W), F32),
            jax.ShapeDtypeStruct((rows, W), F32),
        ),
        in_specs=[pl.BlockSpec(memory_space=pltpu.SMEM), hbm, hbm] + [vmem] * 8,
        out_specs=(vmem, hbm),
        scratch_shapes=[
            pltpu.VMEM((rows, W), BF16),
            pltpu.VMEM((rows, W), BF16),
            pltpu.VMEM((rows, W), BF16),
            pltpu.VMEM((rows, 2 * W), BF16),
            pltpu.VMEM((rows, S), BF16),
            pltpu.VMEM((rows, S), F32),
            pltpu.VMEM((rows, S), F32),
            pltpu.VMEM((rows, 2 * W), BF16),
            pltpu.VMEM((rows, W), F32),
            pltpu.VMEM((rows // CHUNK, 2 * W, CHUNK), BF16),
            pltpu.VMEM((rows // CHUNK, W, CHUNK), BF16),
            pltpu.VMEM((S, 2 * W), F32),
            pltpu.VMEM((8, S), F32),
            pltpu.VMEM((W, W), F32),
            pltpu.VMEM((2 * W, 2 * W), F32),
            pltpu.VMEM((W, S), F32),
            pltpu.VMEM((8, W), F32),
            pltpu.VMEM((8, S), F32),
            pltpu.VMEM((LOW, 24, W), F32),
            pltpu.VMEM((LOW - 1, 24, W), F32),
            pltpu.VMEM((high_n, 24, W), F32),
            pltpu.VMEM((LOW, 24, W), F32),
            pltpu.VMEM((parts * early_rows, W), F32),
            pltpu.VMEM((parts - 1, early_rows, W), F32),
            pltpu.VMEM((high_n, early_rows, W), F32),
            pltpu.VMEM((parts * early_rows, W), F32),
            pltpu.VMEM((parts * late_rows, W), F32),
            pltpu.VMEM((parts - 1, late_rows, W), F32),
            pltpu.VMEM((high_n, late_rows, W), F32),
            pltpu.VMEM((parts * late_rows, W), F32),
            dma((2, rows // CHUNK)),
            dma((rows // CHUNK,)),
            dma((LOW - 1,)), dma((LOW - 1,)),
            dma((high_n - 1,)), dma((high_n - 1,)),
            dma((LOW - 1,)), dma((LOW - 1,)),
            dma((6, max(parts, high_n) - 1)),
            dma((6, max(parts, high_n) - 1)),
        ],
        compiler_params=pltpu.CompilerParams(
            collective_id=0, has_side_effects=True, vmem_limit_bytes=VMEM_LIMIT
        ),
        cost_estimate=pl.CostEstimate(
            flops=flops, bytes_accessed=rows * W * 8, transcendentals=rows * S
        ),
        name="pool_and_gradients",
    )(s, x, g, w1, w2, offset.reshape(1, W), a, wq, wk, wv, w3)

    outs = pl.pallas_call(
        final_kernel,
        out_shape=(
            jax.ShapeDtypeStruct((rows, W), F32),
            jax.ShapeDtypeStruct((W, W), F32),
            jax.ShapeDtypeStruct((W, W), F32),
            jax.ShapeDtypeStruct((1, W), F32),
            jax.ShapeDtypeStruct((D, M), F32),
            jax.ShapeDtypeStruct((1, HEADS), F32),
            jax.ShapeDtypeStruct((D, D), F32),
            jax.ShapeDtypeStruct((D, D), F32),
            jax.ShapeDtypeStruct((D, D), F32),
            jax.ShapeDtypeStruct((W, W), F32),
        ),
        in_specs=[hbm, hbm],
        out_specs=(hbm, hbm, hbm, vmem, hbm, vmem, hbm, hbm, hbm, hbm),
        scratch_shapes=[
            pltpu.VMEM((packed_rows, W), F32),
            pltpu.VMEM((rows, W), F32),
            pltpu.VMEM((D, M), F32),
            pltpu.VMEM((D, D), F32),
            pltpu.VMEM((D, D), F32),
            pltpu.VMEM((D, D), F32),
            dma((PIECES + 1,)), dma((PIECES,)), dma((7,)),
        ],
        compiler_params=pltpu.CompilerParams(vmem_limit_bytes=VMEM_LIMIT),
        cost_estimate=pl.CostEstimate(flops=0, bytes_accessed=rows * W * 8, transcendentals=0),
        name="unpack",
    )(packed, vertex)
    vertex, mid, feature, bias, slices, temp, query, key, value, proj = outs
    return (
        vertex[None], mid, feature, bias.reshape(W), slices, temp.reshape(HEADS),
        query, key, value, proj,
    )


def solution(mesh):
    spread = P("member", "node", None)
    return jax.shard_map(
        functools.partial(shards, mesh.shape["member"], mesh.shape["node"]),
        mesh=mesh,
        in_specs=(spread, spread) + (P(),) * 9,
        out_specs=(spread,) + (P(),) * 9,
        check_vma=False,
    )
```

```python
import functools
import math

import jax
import jax.numpy as jnp
from jax import lax
from jax.experimental import pallas as pl
from jax.experimental.pallas import tpu as pltpu
from jax.sharding import PartitionSpec as P

W = 128
HEADS = 8
M = 32
D = 16
S = HEADS * M
LOW = 4
CHUNK = 2048
EPS = 1e-05
PIECES = 8
VMEM_LIMIT = 62 * 1024 * 1024
F32 = jnp.float32
BF16 = jnp.bfloat16
MESH = pl.DeviceIdType.MESH

NN = (((1,), (0,)), ((), ()))
NT = (((1,), (1,)), ((), ()))
TN = (((0,), (0,)), ((), ()))


def dot(a, b, dims=NN):
    return lax.dot_general(a, b, dims, preferred_element_type=F32)


def split(a):
    upper = a.astype(BF16)
    return upper, (a - upper.astype(F32)).astype(BF16)


def dot32(a, b, dims=NN):
    a_parts = (a,) if a.dtype == BF16 else split(a)
    b_parts = (b,) if b.dtype == BF16 else split(b)
    total = dot(a_parts[0], b_parts[0], dims)
    if len(b_parts) == 2:
        total = total + dot(a_parts[0], b_parts[1], dims)
    if len(a_parts) == 2:
        total = total + dot(a_parts[1], b_parts[0], dims)
    return total


def iota(shape, axis):
    return lax.broadcasted_iota(jnp.int32, shape, axis)


def block_of(index, size):
    return index >> (size.bit_length() - 1)


def group_sum(values, ones):
    return dot(jnp.concatenate(split(values), axis=1), ones)


def fold_rows(a, step):
    total = a[0:step]
    for i in range(step, a.shape[0], step):
        total = total + a[i : i + step]
    return total


def main_kernel(
    n_member, n_node, parts, early_rows, late_rows,
    s_ref, x_hbm, g_hbm, w1_ref, w2_ref, off_ref, a_ref, wq_ref, wk_ref, wv_ref, w3_ref,
    packed_ref, vertex_hbm,
    x_ref, g_ref, mid_ref, fb_ref, pb_ref, probs_ref, mf_ref, vertex_ref,
    gxt_ref, midt_ref,
    pool_acc, den_acc, mid_acc, second_acc, slice_acc, bias_acc,
    pool_src, pool_recv, pool_z, pool_full,
    early_src, early_recv, early_z, early_full, late_src, late_recv, late_z, late_full,
    in_sem, out_sem,
    a_send, a_recv, b_send, b_recv, c_send, c_recv,
    early_sems, late_sems,
):
    rows = x_ref.shape[0]
    high_n = n_node // LOW
    member, node = lax.axis_index("member"), lax.axis_index("node")
    low, high = lax.rem(node, LOW), lax.div(node, LOW)
    group = member * LOW + low

    def low_peer(k):
        return lax.rem(low + k, LOW)

    def high_peer(k):
        return lax.rem(high + k, high_n)

    def group_peer(k):
        return lax.rem(group + k, parts)

    def low_id(k):
        return (member, high * LOW + low_peer(k))

    def high_id(k):
        return (member, high_peer(k) * LOW + low)

    def group_id(k):
        peer = group_peer(k)
        return (lax.div(peer, LOW), high * LOW + lax.rem(peer, LOW))

    def load(i):
        at = pl.ds(pl.multiple_of(i * CHUNK, CHUNK), CHUNK)
        return (
            pltpu.make_async_copy(x_hbm.at[at, :], x_ref.at[at, :], in_sem.at[0, i]),
            pltpu.make_async_copy(g_hbm.at[at, :], g_ref.at[at, :], in_sem.at[1, i]),
        )

    for i in range(rows // CHUNK):
        for copy in load(i):
            copy.start()

    barrier = pltpu.get_barrier_semaphore()
    for k in range(1, parts):
        pl.semaphore_signal(barrier, inc=1, device_id=group_id(k), device_id_type=MESH)
    for k in range(1, high_n):
        pl.semaphore_signal(barrier, inc=1, device_id=high_id(k), device_id_type=MESH)

    def send(src, dst, send_sem, recv_sem, target):
        copy = pltpu.make_async_remote_copy(
            src_ref=src, dst_ref=dst, send_sem=send_sem, recv_sem=recv_sem,
            device_id=target, device_id_type=MESH,
        )
        copy.start()
        return copy

    head_of_slice = block_of(iota((1, S), 1), M)
    inv_s = jnp.zeros((1, S), F32)
    for h in range(HEADS):
        inv_s = jnp.where(head_of_slice == h, 1.0 / jnp.full((1, S), s_ref[h], F32), inv_s)
    inside = block_of(iota((S, S), 0), M) == block_of(iota((S, S), 1), M)
    ones = jnp.where(inside, 1.0, 0.0).astype(BF16)
    ones = jnp.concatenate([ones, ones], axis=0)
    same_head = block_of(iota((W, S), 0), D) == block_of(iota((W, S), 1), M)
    pick_rows = jnp.where((iota((W, D), 0) & (D - 1)) == iota((W, D), 1), 1.0, 0.0).astype(BF16)
    pick_slices = jnp.where((iota((M, S), 1) & (M - 1)) == iota((M, S), 0), 1.0, 0.0).astype(BF16)
    pick_columns = jnp.where((iota((D, W), 1) & (D - 1)) == iota((D, W), 0), 1.0, 0.0).astype(BF16)
    a_all = dot(dot(pick_rows, a_ref[...]).astype(BF16), pick_slices)
    a_block = jnp.where(same_head, a_all, 0.0).astype(BF16)
    head_square = block_of(iota((W, W), 0), D) == block_of(iota((W, W), 1), D)

    def square_block(ref):
        return jnp.where(
            head_square, dot(dot(pick_rows, ref[...]).astype(BF16), pick_columns), 0.0
        ).astype(BF16)

    maps = jnp.concatenate([square_block(r) for r in (wq_ref, wk_ref, wv_ref)], axis=1)
    maps_back = maps.T
    w12 = jnp.concatenate([w1_ref[...], w2_ref[...]], axis=1)
    w12_back = w12.T
    w3_back = w3_ref[...].T
    a_back = a_block.T
    offset = off_ref[...]

    pool_acc[...] = jnp.zeros_like(pool_acc)
    den_acc[...] = jnp.zeros_like(den_acc)

    def first(i, carry):
        for copy in load(i):
            copy.wait()
        at = pl.ds(pl.multiple_of(i * CHUNK, CHUNK), CHUNK)
        x = x_ref[at, :]
        both = dot(x, w12)
        mid = both[:, :W].astype(BF16)
        feat = (both[:, W:] + offset).astype(BF16)
        back = dot(g_ref[at, :], w3_back).astype(BF16)
        logits = dot(mid, a_block) * inv_s
        e = jnp.exp(logits)
        total = group_sum(e, ones)
        guess = pl.reciprocal(total, approx=True)
        probs = e * (guess * (2.0 - total * guess))
        pb = probs.astype(BF16)
        fb = jnp.concatenate([back, feat], axis=1)
        mid_ref[at, :] = mid
        fb_ref[at, :] = fb
        pb_ref[at, :] = pb
        probs_ref[at, :] = probs
        pool_acc[...] += dot(pb, fb, TN)
        den_acc[...] += jnp.sum(probs.reshape(CHUNK // 8, 8, S), axis=0)
        return carry

    lax.fori_loop(0, rows // CHUNK, first, 0)

    slice_head = block_of(iota((S, W), 0), M) == block_of(iota((S, W), 1), D)
    token_grad = fold_rows(jnp.where(slice_head, pool_acc[:, :W], 0.0), M)
    numer = fold_rows(jnp.where(slice_head, pool_acc[:, W:], 0.0), M)
    den = jnp.sum(den_acc[...], axis=0, keepdims=True)
    for p in range(LOW):
        pool_src[p, 0:8, :] = numer[8 * p : 8 * p + 8]
        pool_src[p, 8:16, :] = token_grad[8 * p : 8 * p + 8]
        piece = den[:, (p % 2) * W : (p % 2 + 1) * W]
        pool_src[p, 16:24, :] = jnp.broadcast_to(piece, (8, W))

    pl.semaphore_wait(barrier, parts - 1 + high_n - 1)

    copies = [
        send(pool_src.at[low_peer(k)], pool_recv.at[k - 1], a_send.at[k - 1], a_recv.at[k - 1], low_id(k))
        for k in range(1, LOW)
    ]
    def turn(source, target, start):
        def step(i, carry):
            at = pl.ds(pl.multiple_of(i * CHUNK, CHUNK), CHUNK)
            target[i, start : start + W, :] = source[at, :].T
            return carry

        lax.fori_loop(0, rows // CHUNK, step, 0)

    turn(x_ref, gxt_ref, W)
    total = pool_src[low]
    for k, copy in enumerate(copies):
        copy.wait()
        total = total + pool_recv[k]
    pool_z[high] = total
    copies = [
        send(pool_z.at[high], pool_z.at[high], b_send.at[k - 1], b_recv.at[k - 1], high_id(k))
        for k in range(1, high_n)
    ]
    turn(g_ref, gxt_ref, 0)
    for copy in copies:
        copy.wait()
    total = pool_z[0]
    for k in range(1, high_n):
        total = total + pool_z[k]
    pool_full[low] = total
    copies = [
        send(pool_full.at[low], pool_full.at[low], c_send.at[k - 1], c_recv.at[k - 1], low_id(k))
        for k in range(1, LOW)
    ]
    turn(mid_ref, midt_ref, 0)
    for copy in copies:
        copy.wait()

    numer = jnp.concatenate([pool_full[p, 0:8, :] for p in range(LOW)], axis=0)
    token_grad = jnp.concatenate([pool_full[p, 8:16, :] for p in range(LOW)], axis=0)
    den = jnp.concatenate([pool_full[p, 16:17, :] for p in range(2)], axis=1)
    eye = iota((S, S), 0) == iota((S, S), 1)
    den = jnp.sum(jnp.where(eye, den, 0.0), axis=1, keepdims=True)
    inverse = 1.0 / (den + EPS)
    numer = jnp.where(slice_head, jnp.concatenate([numer] * HEADS, axis=0), 0.0)
    token_grad = jnp.where(slice_head, jnp.concatenate([token_grad] * HEADS, axis=0), 0.0)
    tokens = numer / (den + EPS)
    qkv = dot32(tokens, maps)
    q, k, v = qkv[:, :W], qkv[:, W : 2 * W], qkv[:, 2 * W :]
    scale = 1.0 / math.sqrt(D)
    scores = jnp.where(inside, dot32(q, k, NT) * scale, 0.0)
    e = jnp.where(inside, jnp.exp(scores), 0.0)
    share = e / jnp.sum(e, axis=1, keepdims=True)
    token_out = dot32(share, v).astype(BF16)
    d_share = dot32(token_grad, v, NT)
    d_scores = share * (d_share - jnp.sum(share * d_share, axis=1, keepdims=True)) * scale
    d_qkv = jnp.concatenate(
        [dot32(d_scores, k), dot32(d_scores, q, TN), dot32(share, token_grad, TN)], axis=1
    )
    tok_back = dot32(d_qkv, maps_back)
    numer_back = (tok_back * inverse).astype(BF16)
    den_back = -jnp.sum(tok_back * tokens, axis=1, keepdims=True) * inverse
    den_back = jnp.sum(jnp.where(eye, den_back, 0.0), axis=0, keepdims=True)
    d_maps = dot32(tokens, d_qkv, TN)
    mix = jnp.concatenate([token_out, numer_back], axis=1)
    mix_back = mix.T

    for acc in (mid_acc, second_acc, slice_acc, bias_acc):
        acc[...] = jnp.zeros_like(acc)

    def part(ref, p, size):
        return ref.at[pl.ds(pl.multiple_of(p * size, 8), size), :]

    def start_scatter(src, recv, size, sems):
        return [
            send(part(src, group_peer(k), size), recv.at[k - 1], sems.at[0, k - 1], sems.at[1, k - 1], group_id(k))
            for k in range(1, parts)
        ]

    def start_across(copies, src, recv, z, size, sems):
        total = part(src, group, size)[...]
        for k, copy in enumerate(copies):
            copy.wait()
            total = total + recv[k]
        z[high] = total
        return [
            send(z.at[high], z.at[high], sems.at[2, k - 1], sems.at[3, k - 1], high_id(k))
            for k in range(1, high_n)
        ]

    def start_gather(copies, z, full, size, sems):
        for copy in copies:
            copy.wait()
        total = z[0]
        for k in range(1, high_n):
            total = total + z[k]
        mine = part(full, group, size)
        mine[...] = total
        return [
            send(mine, mine, sems.at[4, k - 1], sems.at[5, k - 1], group_id(k))
            for k in range(1, parts)
        ]

    def second(i, carry):
        at = pl.ds(pl.multiple_of(i * CHUNK, CHUNK), CHUNK)
        both = dot(pb_ref[at, :], mix)
        rounded = both.astype(BF16)
        feat_back = both[:, W:]
        mf_ref[at, W:] = rounded[:, W:]
        bias_acc[...] += jnp.sum(feat_back.reshape(CHUNK // 8, 8, W), axis=0)
        second_acc[...] += dot(gxt_ref[i], rounded)
        return carry

    def third(i, carry):
        at = pl.ds(pl.multiple_of(i * CHUNK, CHUNK), CHUNK)
        probs = probs_ref[at, :]
        prob_back = dot(fb_ref[at, :], mix_back) + den_back
        inner = group_sum(probs * prob_back, ones)
        logit_back = probs * (prob_back - inner)
        score_back = (logit_back * inv_s).astype(BF16)
        mid_back = dot(score_back, a_back).astype(BF16)
        mf_ref[at, :W] = mid_back
        mid_acc[...] += dot(gxt_ref[i, W:, :], mid_back)
        slice_acc[...] += dot(midt_ref[i], score_back)
        return carry

    steps = rows // CHUNK
    lax.fori_loop(0, steps, second, 0)
    early_src[0:W, :] = second_acc[W:, W:]
    early_src[W : 2 * W, :] = second_acc[:W, :W].T
    early = start_scatter(early_src, early_recv, early_rows, early_sems)
    lax.fori_loop(0, steps // 2, third, 0)
    early = start_across(early, early_src, early_recv, early_z, early_rows, early_sems)
    lax.fori_loop(steps // 2, steps, third, 0)
    early = start_gather(early, early_z, early_full, early_rows, early_sems)

    late_src[0:W, :] = mid_acc[...]
    slices = jnp.where(same_head, slice_acc[...], 0.0)
    temp = fold_rows(slices * a_block.astype(F32), 8) * -inv_s
    slices = fold_rows(slices, D)
    slices = slices[:, :W] + slices[:, W:]
    slices = slices + pltpu.roll(slices, 64, 1)
    slices = slices + pltpu.roll(slices, 32, 1)
    lane = iota((D, W), 1)
    owner = (node == 0).astype(F32)
    block = jnp.where(lane < M, slices, 0.0)
    for i in range(3):
        term = fold_rows(d_maps[:, i * W : (i + 1) * W], D)
        for shift in (64, 32, 16):
            term = term + pltpu.roll(term, shift, 1)
        start = M + i * D
        block = jnp.where((lane >= start) & (lane < start + D), term * owner, block)
    late_src[W : W + D, :] = block
    pick_heads = jnp.where(block_of(iota((S, W), 0), M) == iota((S, W), 1), 1.0, 0.0).astype(BF16)
    temp = jnp.sum(dot32(temp, pick_heads), axis=0, keepdims=True)
    bias = jnp.sum(bias_acc[...], axis=0, keepdims=True)
    row = iota((8, W), 0)
    late_src[W + D : W + D + 8, :] = jnp.where(row == 0, bias, jnp.where(row == 1, temp, 0.0))
    used = W + D + 8
    if used < parts * late_rows:
        late_src[used:, :] = jnp.zeros((parts * late_rows - used, W), F32)

    late = start_scatter(late_src, late_recv, late_rows, late_sems)

    def store(i):
        at = pl.ds(pl.multiple_of(i * CHUNK, CHUNK), CHUNK)
        return pltpu.make_async_copy(vertex_ref.at[at, :], vertex_hbm.at[at, :], out_sem.at[i])

    def fourth(i, carry):
        at = pl.ds(pl.multiple_of(i * CHUNK, CHUNK), CHUNK)
        vertex_ref[at, :] = dot(mf_ref[at, :], w12_back)
        store(i).start()
        return carry

    lax.fori_loop(0, steps // 2, fourth, 0)
    late = start_across(late, late_src, late_recv, late_z, late_rows, late_sems)
    lax.fori_loop(steps // 2, steps, fourth, 0)
    late = start_gather(late, late_z, late_full, late_rows, late_sems)
    for copy in early:
        copy.wait()
    packed_ref[0 : 2 * W, :] = early_full[...]
    for copy in late:
        copy.wait()
    packed_ref[2 * W :, :] = late_full[...]
    for i in range(steps):
        store(i).wait()


def final_kernel(
    packed_ref, vertex_ref,
    out_ref, mid_ref, feature_ref, bias_ref, slice_ref, temp_ref, query_ref, key_ref, value_ref, proj_ref,
    packed, held, slice_out, query_out, key_out, value_out, load_sems, store_sems, small_sems,
):
    size = vertex_ref.shape[0] // PIECES
    pieces = [pl.ds(i * size, size) for i in range(PIECES)]
    loads = [
        pltpu.make_async_copy(vertex_ref.at[at, :], held.at[at, :], load_sems.at[i])
        for i, at in enumerate(pieces)
    ]
    copies = [
        pltpu.make_async_copy(held.at[at, :], out_ref.at[at, :], store_sems.at[i])
        for i, at in enumerate(pieces)
    ]
    load_packed = pltpu.make_async_copy(packed_ref, packed, load_sems.at[PIECES])
    load_packed.start()
    for copy in loads:
        copy.start()
    load_packed.wait()
    block = packed[3 * W : 3 * W + D, :]
    slice_out[...] = block[:, 0:M]
    query_out[...] = block[:, M : M + D]
    key_out[...] = block[:, M + D : M + 2 * D]
    value_out[...] = block[:, M + 2 * D : M + 3 * D]
    last = 3 * W + D
    bias_ref[...] = packed[last : last + 1, :]
    temp_ref[...] = packed[last + 1 : last + 2, 0:HEADS]
    smalls = [
        (packed.at[0:W, :], feature_ref),
        (packed.at[W : 2 * W, :], proj_ref),
        (packed.at[2 * W : 3 * W, :], mid_ref),
        (slice_out, slice_ref),
        (query_out, query_ref),
        (key_out, key_ref),
        (value_out, value_ref),
    ]
    smalls = [
        pltpu.make_async_copy(source, target, small_sems.at[i])
        for i, (source, target) in enumerate(smalls)
    ]
    for copy in smalls:
        copy.start()
    for before, copy in zip(loads, copies):
        before.wait()
        copy.start()
    for copy in smalls + copies:
        copy.wait()


def shards(n_member, n_node, x, g, w1, w2, offset, a, s, wq, wk, wv, w3):
    x, g = x[0], g[0]
    rows = x.shape[0]
    high_n = n_node // LOW
    parts = n_member * LOW
    early_rows = -(-2 * W // (8 * parts)) * 8
    late_rows = -(-(W + D + 8) // (8 * parts)) * 8
    packed_rows = 2 * W + parts * late_rows
    assert parts * early_rows == 2 * W and n_node % LOW == 0
    vmem = pl.BlockSpec(memory_space=pltpu.VMEM)
    hbm = pl.BlockSpec(memory_space=pl.ANY)
    dma = pltpu.SemaphoreType.DMA
    flops = 2 * rows * S * S * 12
    packed, vertex = pl.pallas_call(
        functools.partial(main_kernel, n_member, n_node, parts, early_rows, late_rows),
        out_shape=(
            jax.ShapeDtypeStruct((packed_rows, W), F32),
            jax.ShapeDtypeStruct((rows, W), F32),
        ),
        in_specs=[pl.BlockSpec(memory_space=pltpu.SMEM), hbm, hbm] + [vmem] * 8,
        out_specs=(vmem, hbm),
        scratch_shapes=[
            pltpu.VMEM((rows, W), BF16),
            pltpu.VMEM((rows, W), BF16),
            pltpu.VMEM((rows, W), BF16),
            pltpu.VMEM((rows, 2 * W), BF16),
            pltpu.VMEM((rows, S), BF16),
            pltpu.VMEM((rows, S), F32),
            pltpu.VMEM((rows, 2 * W), BF16),
            pltpu.VMEM((rows, W), F32),
            pltpu.VMEM((rows // CHUNK, 2 * W, CHUNK), BF16),
            pltpu.VMEM((rows // CHUNK, W, CHUNK), BF16),
            pltpu.VMEM((S, 2 * W), F32),
            pltpu.VMEM((8, S), F32),
            pltpu.VMEM((W, W), F32),
            pltpu.VMEM((2 * W, 2 * W), F32),
            pltpu.VMEM((W, S), F32),
            pltpu.VMEM((8, W), F32),
            pltpu.VMEM((LOW, 24, W), F32),
            pltpu.VMEM((LOW - 1, 24, W), F32),
            pltpu.VMEM((high_n, 24, W), F32),
            pltpu.VMEM((LOW, 24, W), F32),
            pltpu.VMEM((parts * early_rows, W), F32),
            pltpu.VMEM((parts - 1, early_rows, W), F32),
            pltpu.VMEM((high_n, early_rows, W), F32),
            pltpu.VMEM((parts * early_rows, W), F32),
            pltpu.VMEM((parts * late_rows, W), F32),
            pltpu.VMEM((parts - 1, late_rows, W), F32),
            pltpu.VMEM((high_n, late_rows, W), F32),
            pltpu.VMEM((parts * late_rows, W), F32),
            dma((2, rows // CHUNK)),
            dma((rows // CHUNK,)),
            dma((LOW - 1,)), dma((LOW - 1,)),
            dma((high_n - 1,)), dma((high_n - 1,)),
            dma((LOW - 1,)), dma((LOW - 1,)),
            dma((6, max(parts, high_n) - 1)),
            dma((6, max(parts, high_n) - 1)),
        ],
        compiler_params=pltpu.CompilerParams(
            collective_id=0, has_side_effects=True, vmem_limit_bytes=VMEM_LIMIT
        ),
        cost_estimate=pl.CostEstimate(
            flops=flops, bytes_accessed=rows * W * 8, transcendentals=rows * S
        ),
        name="pool_and_gradients",
    )(s, x, g, w1, w2, offset.reshape(1, W), a, wq, wk, wv, w3)

    outs = pl.pallas_call(
        final_kernel,
        out_shape=(
            jax.ShapeDtypeStruct((rows, W), F32),
            jax.ShapeDtypeStruct((W, W), F32),
            jax.ShapeDtypeStruct((W, W), F32),
            jax.ShapeDtypeStruct((1, W), F32),
            jax.ShapeDtypeStruct((D, M), F32),
            jax.ShapeDtypeStruct((1, HEADS), F32),
            jax.ShapeDtypeStruct((D, D), F32),
            jax.ShapeDtypeStruct((D, D), F32),
            jax.ShapeDtypeStruct((D, D), F32),
            jax.ShapeDtypeStruct((W, W), F32),
        ),
        in_specs=[hbm, hbm],
        out_specs=(hbm, hbm, hbm, vmem, hbm, vmem, hbm, hbm, hbm, hbm),
        scratch_shapes=[
            pltpu.VMEM((packed_rows, W), F32),
            pltpu.VMEM((rows, W), F32),
            pltpu.VMEM((D, M), F32),
            pltpu.VMEM((D, D), F32),
            pltpu.VMEM((D, D), F32),
            pltpu.VMEM((D, D), F32),
            dma((PIECES + 1,)), dma((PIECES,)), dma((7,)),
        ],
        compiler_params=pltpu.CompilerParams(vmem_limit_bytes=VMEM_LIMIT),
        cost_estimate=pl.CostEstimate(flops=0, bytes_accessed=rows * W * 8, transcendentals=0),
        name="unpack",
    )(packed, vertex)
    vertex, mid, feature, bias, slices, temp, query, key, value, proj = outs
    return (
        vertex[None], mid, feature, bias.reshape(W), slices, temp.reshape(HEADS),
        query, key, value, proj,
    )


def solution(mesh):
    spread = P("member", "node", None)
    return jax.shard_map(
        functools.partial(shards, mesh.shape["member"], mesh.shape["node"]),
        mesh=mesh,
        in_specs=(spread, spread) + (P(),) * 9,
        out_specs=(spread,) + (P(),) * 9,
        check_vma=False,
    )
```
